32 devices in a mesh: seq: 8 (over y, x, core), mp: 4 (over z).
Axes of the slice: x: 2, y: 2, z: 4, core: 2. Of those that a mesh axis runs over, the one named last changes fastest.
Arguments:
- qkv: bfloat16 [3, 8192, 8192], P(None, 'mp', 'seq'), may hold values from -6 to 6
- short_taps: bfloat16 [3, 8192, 7], P(None, 'mp'), may hold values from -2 to 2
- medium_taps: bfloat16 [8192, 128], P('mp'), may hold values from -0.5 to 0.5
- skip_gain: float32 [8192], P('mp'), may hold values from -4 to 4
- w_out: bfloat16 [8192, 8192], P('mp'), may hold values from -0.09375 to 0.09375
- resid: bfloat16 [8192, 8192], P('mp', 'seq'), may hold values from -6 to 6
- steer: float32 [8192], P('mp'), may hold values from -5 to 5
Outputs:
- layer_out: bfloat16 [8192, 8192], P('mp', 'seq')
The draws below stay inside these ranges and needn't reach their ends.
All inputs are finite; a program needn't handle non-finite values.
Results may differ from the reference program's by a relative error of at most 0.017.
Values may be sent and summed in bfloat16 or wider, within the bound.
A program may use at most 192 MiB of HBM per device.

```python
import jax
import jax.numpy as jnp
from jax import lax

D = 8192
STAPS = 7
MTAPS = 128
LEN = 8192
N_MP = 4


def spiked(values, own_key, source, target, parts, factor):
    def block_of(dim):
        return (jnp.arange(values.shape[dim]) // (values.shape[dim] // parts)).reshape((-1,) + (1,) * (values.ndim - 1 - dim))

    near = jax.random.permutation(own_key, parts)[block_of(target)]
    far = (block_of(target) + parts // 2) % parts
    return jnp.where((block_of(source) == near) | (block_of(source) == far), factor * values, values)


def levels(own_key, dims, cuts, low, high):
    loudness = 1.0
    for position, parts in cuts:
        heights = jax.random.uniform(jax.random.fold_in(jax.random.fold_in(own_key, 6), position), (parts,), jnp.float32, low / len(cuts), high / len(cuts))
        loudness = loudness * jnp.repeat(jnp.exp(heights), dims[position] // parts).reshape((-1,) + (1,) * (len(dims) - 1 - position))
    return loudness


def noise(own_key, extent, width, limit, pieces=(), held_as=jnp.bfloat16):
    entries = jax.random.normal(own_key, extent, jnp.float32) * width
    if len(pieces) > 0:
        entries = levels(own_key, extent, pieces, -0.22, 0.18) * entries
    return jnp.clip(entries, min=-limit, max=limit).astype(held_as)


def heavy_noise(stream_key, dims, spread, most, pieces, heavy, kind=jnp.bfloat16):
    entries = spread * jax.random.normal(stream_key, dims, jnp.float32)
    if pieces:
        entries = entries * levels(stream_key, dims, pieces, -0.22, 0.18)
    return jnp.clip(spiked(entries, jax.random.fold_in(stream_key, 3), *heavy), -most, most).astype(kind)


def setup_inputs(seed: int = 0) -> dict:
    key_list = jax.random.split(jax.random.key(seed), 8)
    return {
        "qkv": noise(key_list[0], (3, D, LEN), 1.0, 6.0, ((1, 4), (2, 8))),
        "short_taps": noise(key_list[1], (3, D, STAPS), STAPS ** -0.5, 2.0, ((1, 4),)),
        "medium_taps": noise(key_list[2], (D, MTAPS), MTAPS ** -0.5, 0.5, ((0, 4),)),
        "skip_gain": noise(key_list[3], (D,), 1.0, 4.0, ((0, 4),), jnp.float32),
        "w_out": heavy_noise(key_list[4], (D, D), D ** -0.5, 0.09375, ((0, 4),), (0, 1, 4, 2.0)),
        "resid": noise(key_list[5], (D, LEN), 1.0, 6.0, ((0, 4), (1, 8))),
        "steer": noise(key_list[6], (D,), 1.0, 5.0, ((0, 4),), jnp.float32),
    }


def short_conv(x, taps):
    length = x.shape[1]
    padded = jnp.pad(x, ((0, 0), (STAPS - 1, 0)))
    total = jnp.zeros_like(x)
    for j in range(STAPS):
        total = total + taps[:, j:j + 1] * padded[:, STAPS - 1 - j:STAPS - 1 - j + length]
    return total


def medium_block(pair):
    values, filt = pair
    length = values.shape[1]
    padded = jnp.pad(values, ((0, 0), (MTAPS - 1, 0)))

    def add_tap(j, total):
        column = lax.dynamic_slice_in_dim(filt, j, 1, 1)
        window = lax.dynamic_slice_in_dim(padded, MTAPS - 1 - j, length, 1)
        return total + column * window

    return lax.fori_loop(0, MTAPS, add_tap, jnp.zeros_like(values))


def reference(qkv, short_taps, medium_taps, skip_gain, w_out, resid, steer):
    f32 = jnp.float32
    taps = short_taps.astype(f32)
    q_filt = short_conv(qkv[0].astype(f32), taps[0])
    k_filt = short_conv(qkv[1].astype(f32), taps[1])
    v_filt = short_conv(qkv[2].astype(f32), taps[2])
    kv = (k_filt * v_filt).astype(jnp.bfloat16)
    kv_wide = kv.astype(f32)
    block = min(D, 256)
    length = kv.shape[1]
    blocks = lax.map(medium_block, (kv_wide.reshape(D // block, block, length), medium_taps.astype(f32).reshape(D // block, block, MTAPS)))
    med = blocks.reshape(D, length) + skip_gain.astype(f32)[:, None] * kv_wide
    y_out = (q_filt * med).astype(jnp.bfloat16)
    group = D // N_MP

    def add_group(g, total):
        y_part = lax.dynamic_slice_in_dim(y_out, g * group, group, 0).astype(f32)
        w_part = lax.dynamic_slice_in_dim(w_out, g * group, group, 0).astype(f32)
        part = jnp.dot(w_part.T, y_part, precision=lax.Precision.HIGHEST)
        rounded = lax.optimization_barrier(part.astype(jnp.bfloat16))
        return total + rounded.astype(f32)

    proj = lax.fori_loop(0, N_MP, add_group, jnp.zeros((D, length), f32))
    return (resid.astype(f32) + proj + steer.astype(f32)[:, None]).astype(jnp.bfloat16)
```

```python
import functools

import jax
import jax.numpy as jnp
from jax import lax
from jax.experimental import pallas as pl
from jax.experimental.pallas import tpu as pltpu
from jax.sharding import PartitionSpec as P

STAPS = 7
MTAPS = 128
LANES = 128
F32 = jnp.float32
BF16 = jnp.bfloat16
MESH = pl.DeviceIdType.MESH


def from_behind(value, axis, steps):
    count = lax.axis_size(axis)
    return lax.ppermute(value, axis, [(source, source + steps) for source in range(count - steps)])


def chunks(slab):
    sizes = [1]
    left = slab // LANES - 3
    while left > 0:
        sizes.append(min(left, 2 if len(sizes) == 1 else 3))
        left -= sizes[-1]
    sizes.append(2)
    plan, end = [], slab
    for size in sizes:
        end -= size * LANES
        plan.append((end, size * LANES))
    return plan


def feature_kernel(blocks, *refs):
    token_refs = refs[:blocks]
    short_ref, medium_ref, y_ref, wide, kv = refs[blocks:]
    for at, ref in enumerate(token_refs):
        for s in range(3):
            if s > 0 or at > 0:
                wide[s, at * LANES : (at + 1) * LANES] = ref[s].astype(F32).T

    def short(s, row):
        total = short_ref[s, 0:1] * wide[s, row : row + LANES]
        for j in range(1, STAPS):
            total = total + short_ref[s, j : j + 1] * wide[s, row - j : row - j + LANES]
        return total

    for at in range(1, blocks):
        row = at * LANES
        kv[row - LANES : row] = (short(1, row) * short(2, row)).astype(BF16).astype(F32)

    for at in range(blocks - 2):
        row = at * LANES
        total = jnp.zeros((LANES, LANES), F32)
        for low in range(8):
            start = row + 8 - low
            block = kv[start : start + LANES + MTAPS - 8]
            for high in range(0, MTAPS, 8):
                first = MTAPS - 8 - high
                total = total + medium_ref[high + low : high + low + 1] * block[first : first + LANES]
        y_ref[row : row + LANES] = (short(0, row + 2 * LANES) * total).astype(BF16)


def features(sources, short, medium):
    channels = short.shape[2]
    blocks = len(sources)
    tokens = (blocks - 2) * LANES
    return pl.pallas_call(
        functools.partial(feature_kernel, blocks),
        grid=(channels // LANES,),
        in_specs=[pl.BlockSpec((3, LANES, LANES), lambda c, at=at: (0, c, at)) for _, at in sources]
        + [
            pl.BlockSpec((3, STAPS, LANES), lambda c: (0, 0, c)),
            pl.BlockSpec((MTAPS, LANES), lambda c: (0, c)),
        ],
        out_specs=pl.BlockSpec((tokens, LANES), lambda c: (0, c)),
        out_shape=jax.ShapeDtypeStruct((tokens, channels), BF16),
        scratch_shapes=[
            pltpu.VMEM((3, blocks * LANES, LANES), F32),
            pltpu.VMEM(((blocks - 1) * LANES, LANES), F32),
        ],
        cost_estimate=pl.CostEstimate(
            flops=2 * channels * tokens * (MTAPS + 4 * STAPS),
            bytes_accessed=6 * channels * blocks * LANES,
            transcendentals=0,
        ),
    )(*[array for array, _ in sources], short, medium)


def finish_kernel(*refs):
    resid_ref, steer_ref, proj_ref, out_ref = refs[0], refs[1], refs[2], refs[-1]
    gain = proj_ref[...].astype(F32) + steer_ref[...]
    out_ref[...] = (resid_ref[...].astype(F32) + gain.T).astype(BF16)


def finish(resid, steer, proj, out, first):
    tokens, channels = proj.shape
    rows = min(channels, 1024)
    at = first // LANES
    column = pl.BlockSpec((rows, LANES), lambda t, c: (c, at + t))
    specs = [
        column,
        pl.BlockSpec((1, rows), lambda t, c: (0, c)),
        pl.BlockSpec((LANES, rows), lambda t, c: (t, c)),
    ]
    held = [] if out is None else [out]
    return pl.pallas_call(
        finish_kernel,
        grid=(tokens // LANES, channels // rows),
        in_specs=specs + [pl.BlockSpec(memory_space=pl.ANY)] * len(held),
        out_specs=column,
        out_shape=jax.ShapeDtypeStruct(resid.shape, BF16),
        input_output_aliases={3: 0} if held else {},
        cost_estimate=pl.CostEstimate(
            flops=2 * channels * tokens, bytes_accessed=6 * channels * tokens, transcendentals=0
        ),
    )(resid, steer, proj, *held)


def shards(qkv, short_taps, medium_taps, skip_gain, w_out, resid, steer):
    slab = qkv.shape[2]
    short = jnp.swapaxes(short_taps.astype(F32), 1, 2)
    medium = medium_taps.astype(F32)
    medium = jnp.concatenate([medium[:, :1] + skip_gain[:, None], medium[:, 1:]], 1).T
    rim = from_behind(qkv[:, :, slab - 2 * LANES :], "seq", 1)
    out = None
    projs = []
    for first, tokens in chunks(slab):
        at = first // LANES
        sources = [(rim, i + 2) if i < 0 else (qkv, i) for i in range(at - 2, at + tokens // LANES)]
        y = features(sources, short, medium)
        part = jnp.dot(y, w_out, preferred_element_type=F32).astype(BF16)
        proj = lax.psum_scatter(part, "mp", scatter_dimension=1, tiled=True)
        projs.append((first, proj))
    for first, proj in projs:
        out = finish(resid, steer[None], proj, out, first)
    return out


PHASE = MTAPS // 4
EDGE = 8
COLS = 512
VMEM_LIMIT = 62 << 20
FEATURES = ((896, 128), (768, 128), (512, 256), (256, 256), (0, 256))
PARTS = ((896, 128), (768, 128), (512, 256), (256, 256), (128, 128), (0, 128))
PLANE = (2, 4, 6)
SUM_IN, Y_IN, ACROSS_OUTER, ACROSS_INNER, SUM_OUT = range(5)


def nine_taps(medium):
    phase = [medium[i::4] for i in range(4)]
    even = [phase[0], phase[2], phase[0] + phase[2]]
    odd = [phase[1], phase[3], phase[1] + phase[3]]
    return jnp.concatenate(even + odd + [a + b for a, b in zip(even, odd)], 0)


def filtered(blocks, short_ref, nine_ref, lanes, wide, kv, xs, back, med):
    count = (blocks - 2) * LANES // 4
    held = (blocks - 1) * LANES // 4

    def short(s, row):
        total = short_ref[s, 0:1, lanes] * wide[s, row : row + LANES]
        for j in range(1, STAPS):
            total = total + short_ref[s, j : j + 1, lanes] * wide[s, row - j : row - j + LANES]
        return total

    for at in range(1, blocks):
        row = at * LANES
        kv[row - LANES : row] = (short(1, row) * short(2, row)).astype(BF16).astype(F32)
    phase = [kv[pl.ds(p, held, stride=4)] for p in range(4)]
    even = [phase[0], phase[2], phase[0] + phase[2]]
    odd = [phase[1], phase[3], phase[1] + phase[3]]
    for i, x in enumerate(even + odd + [a + b for a, b in zip(even, odd)]):
        xs[i, EDGE : EDGE + held] = x

    def conv(i, edge):
        size, total = count + edge, None
        for low in range(8):
            start = EDGE + 8 - edge - low
            block = xs[i, start : start + size + PHASE - 8]
            for high in range(0, PHASE, 8):
                first = PHASE - 8 - high
                tap = i * PHASE + high + low
                term = nine_ref[tap : tap + 1, lanes] * block[first : first + size]
                total = term if total is None else total + term
        return total

    def delayed(value):
        back[0 : count + EDGE] = value
        return back[EDGE - 1 : EDGE - 1 + count]

    def pair(g, edge):
        first, second, both = conv(3 * g, edge), conv(3 * g + 1, EDGE), conv(3 * g + 2, edge)
        return first[edge:] + delayed(second), both - first - second[EDGE - edge :]

    odd0, odd1 = pair(1, EDGE)
    late, odd1 = delayed(odd1), odd1[EDGE:]
    even0, even1 = pair(0, 0)
    both0, both1 = pair(2, 0)
    med[pl.ds(0, count, stride=4)] = even0 + late
    med[pl.ds(1, count, stride=4)] = both0 - even0 - odd0
    med[pl.ds(2, count, stride=4)] = even1 + odd0
    med[pl.ds(3, count, stride=4)] = both1 - even1 - odd1
    for at in range(blocks - 2):
        row = at * LANES
        yield row, (short(0, row + 2 * LANES) * med[row : row + LANES]).astype(BF16)


def line_kernel(
    qkv, w_out, resid, short_ref, nine_ref, steer_ref,
    out, wx_far, wx_near, rim,
    y, yx, st1, st2, st3, r1, rp, rq, wbuf, qbuf, rbuf, wide, kv, xs, back, med,
    send, recv, w_send, w_recv, rim_send, rim_recv, fetch_sem, q_sem, r_sem,
):
    s, m = lax.axis_index("seq"), lax.axis_index("mp")
    channels, slab = qkv.shape[1], qkv.shape[2]
    width = resid.shape[0]
    steps = width // COLS
    low = m < 2
    inner = jnp.logical_or(m == 1, m == 2)
    outer = jnp.logical_not(inner)
    far_outer, far_inner = jnp.where(low, 3, 0), jnp.where(low, 2, 1)
    near_inner, near_outer = jnp.where(low, 1, 2), jnp.where(low, 0, 3)
    inward = (s, near_inner)
    outward = (s, near_outer)
    opposite = (s, jnp.where(low, 2, 1))

    barrier = pltpu.get_barrier_semaphore()

    def greet(condition, device):
        @pl.when(condition)
        def _():
            pl.semaphore_signal(barrier, inc=1, device_id=device, device_id_type=MESH)

    greet(m < 3, (s, jnp.minimum(m + 1, 3)))
    greet(m > 0, (s, jnp.maximum(m - 1, 0)))
    greet(s < 7, (jnp.minimum(s + 1, 7), m))
    greet(s > 0, (jnp.maximum(s - 1, 0), m))
    for flip in (1, *PLANE):
        pl.semaphore_signal(barrier, inc=1, device_id=(s ^ flip, m), device_id_type=MESH)
    one = lambda c: jnp.where(c, 1, 0)
    pl.semaphore_wait(barrier, 4 + one(m < 3) + one(m > 0) + one(s < 7) + one(s > 0))

    def remote(src, dst, sent, got, device):
        return pltpu.make_async_remote_copy(
            src_ref=src, dst_ref=dst, send_sem=sent, recv_sem=got, device_id=device, device_id_type=MESH
        )

    rim_copy = remote(qkv.at[:, :, slab - 256 : slab], rim, rim_send, rim_recv, (jnp.minimum(s + 1, 7), m))
    pl.when(s < 7)(rim_copy.start)

    share = channels // 8
    held = (wx_far, wx_near)

    def rows_of(device):
        return pl.ds(pl.multiple_of(device * share, share), share)

    def w_inward(g):
        group = (far_inner, near_inner)[g]
        columns = pl.ds(pl.multiple_of(group * width, width), width)
        return remote(
            w_out.at[rows_of(s), columns], held[g].at[rows_of(s)], w_send.at[g, 0], w_recv.at[g, 0], inward
        )

    def w_plane(g, i):
        mine = held[g].at[rows_of(s)]
        return remote(mine, mine, w_send.at[g, 1 + i], w_recv.at[g, 1 + i], (s ^ PLANE[i], m))

    def w_core(g, i):
        piece = held[g].at[rows_of(s if i == 0 else s ^ PLANE[i - 1])]
        return remote(piece, piece, w_send.at[g, 4 + i], w_recv.at[g, 4 + i], (s ^ 1, m))

    def relay_plane(g):
        w_inward(g).wait_recv()
        for i in range(3):
            w_plane(g, i).start()
        w_core(g, 0).start()

    def relay_core(g):
        for i in range(3):
            w_plane(g, i).wait_recv()
            w_core(g, 1 + i).start()

    def relay_end(g):
        for i in range(4):
            w_core(g, i).wait_recv()

    def rows(k):
        return pl.ds(PARTS[k][0], PARTS[k][1])

    def moving(kind, k):
        src, dst, device = {
            SUM_IN: (st1, r1, inward),
            Y_IN: (y, yx, inward),
            ACROSS_OUTER: (st1, rp, opposite),
            ACROSS_INNER: (st2, rq, opposite),
            SUM_OUT: (st3, r1, outward),
        }[kind]
        return remote(src.at[rows(k)], dst.at[rows(k)], send.at[kind, k], recv.at[kind, k], device)

    def fetch(which, half, j):
        if which in (0, 1):
            block = held[which].at[:, pl.ds(pl.multiple_of(j * COLS, COLS), COLS)]
        else:
            group = {"fo": far_outer, "fi": far_inner, "ni": near_inner, "no": near_outer}[which]
            block = w_out.at[:, pl.ds(pl.multiple_of(group * width + j * COLS, COLS), COLS)]
        return pltpu.make_async_copy(block, wbuf.at[half, j], fetch_sem.at[half, j])

    class Plan:
        def __init__(self, units):
            self.units, self.at, self.ended = units, 0, set()

        def load(self, i):
            if i < len(self.units):
                which = self.units[i]
                if which in (0, 1) and which not in self.ended:
                    self.ended.add(which)
                    relay_end(which)
                for j in range(steps):
                    fetch(which, i % 2, j).start()

        def run(self, src, parts, each):
            i = self.at
            self.at += 1
            self.load(i + 1)
            first = PARTS[parts[-1]][0]
            tokens = sum(PARTS[k][1] for k in parts)

            def body(j, carry):
                fetch(self.units[i], i % 2, j).wait()
                total = jnp.dot(src[first : first + tokens], wbuf[i % 2, j], preferred_element_type=F32)
                each(total, j, pl.ds(first, tokens), pl.ds(pl.multiple_of(j * COLS, COLS), COLS))
                return carry

            lax.fori_loop(0, steps, body, 0)

    def put(dst, *adds):
        def each(total, j, at, columns):
            for ref in adds:
                total = total + ref[at, columns].astype(F32)
            dst[at, columns] = total.astype(BF16)

        return each

    def resid_in(slot, first, tokens):
        return pltpu.make_async_copy(
            resid.at[:, first : first + tokens], rbuf.at[slot, :, 0:tokens], r_sem.at[0, slot]
        )

    def out_of(slot, first, tokens):
        return pltpu.make_async_copy(
            rbuf.at[slot, :, 0:tokens], out.at[:, first : first + tokens], r_sem.at[1, slot]
        )

    leaving = []

    def final(plan, src, parts, ref):
        first = PARTS[parts[-1]][0]
        tokens = sum(PARTS[k][1] for k in parts)
        slot = len(leaving) % 2
        if len(leaving) >= 2:
            out_of(*leaving[-2]).wait()
        resid_in(slot, first, tokens).start()
        leaving.append((slot, first, tokens))

        def each(total, j, at, columns):
            @pl.when(j == 0)
            def _():
                resid_in(slot, first, tokens).wait()

            total = total + ref[at, columns].astype(F32) + steer_ref[0:1, columns]
            rbuf[slot, columns, 0:tokens] = (
                rbuf[slot, columns, 0:tokens].astype(F32) + total.T
            ).astype(BF16)

        plan.run(src, parts, each)
        out_of(slot, first, tokens).start()

    def settle():
        for left in leaving[-2:]:
            out_of(*left).wait()
        leaving.clear()

    def feature(k):
        first, tokens = FEATURES[k]
        span = tokens + 256

        def load(c, slot, act):
            lanes = pl.ds(pl.multiple_of(c * LANES, LANES), LANES)
            if first > 0:
                act(pltpu.make_async_copy(
                    qkv.at[:, lanes, first - 256 : first + tokens], qbuf.at[slot, :, :, 0:span], q_sem.at[0, slot]
                ))
            else:
                act(pltpu.make_async_copy(
                    qkv.at[:, lanes, 0:tokens], qbuf.at[slot, :, :, 256:span], q_sem.at[0, slot]
                ))

                @pl.when(s > 0)
                def _():
                    act(pltpu.make_async_copy(rim.at[:, lanes], qbuf.at[slot, :, :, 0:256], q_sem.at[1, slot]))

        if first == 0:

            @pl.when(s > 0)
            def _():
                rim_copy.wait_recv()

            @pl.when(s == 0)
            def _():
                qbuf[:, :, :, 0:256] = jnp.zeros((2, 3, LANES, 256), BF16)

        load(0, 0, lambda copy: copy.start())
        count = channels // LANES

        def body(c, carry):
            slot = lax.rem(c, 2)

            @pl.when(c + 1 < count)
            def _():
                load(c + 1, 1 - slot, lambda copy: copy.start())

            load(c, slot, lambda copy: copy.wait())
            lanes = pl.ds(pl.multiple_of(c * LANES, LANES), LANES)
            for at in range(span // LANES):
                for i in range(3):
                    if i > 0 or at > 0:
                        wide[i, at * LANES : (at + 1) * LANES] = (
                            qbuf[slot, i, :, at * LANES : (at + 1) * LANES].astype(F32).T
                        )
            for row, value in filtered(span // LANES, short_ref, nine_ref, lanes, wide, kv, xs, back, med):
                y[first + row : first + row + LANES, lanes] = value
            return carry

        lax.fori_loop(0, count, body, 0)

    def wait_in(kind, *parts):
        for k in parts:
            moving(kind, k).wait_recv()

    def go(kind, *parts):
        for k in parts:
            moving(kind, k).start()

    class Inner:
        def __init__(self, plan):
            self.plan = plan

        def cross(self, *parts):
            wait_in(SUM_IN, *parts)
            self.plan.run(y, parts, put(st1, r1))
            go(ACROSS_OUTER, *parts)

        def far(self, *parts):
            self.plan.run(y, parts, put(st2))

        def far_end(self, *parts):
            wait_in(Y_IN, *parts)
            self.plan.run(yx, parts, put(st2, st2))
            go(ACROSS_INNER, *parts)

        def out(self, *parts):
            wait_in(ACROSS_OUTER, *parts)
            self.plan.run(y, parts, put(st3, rp))
            go(SUM_OUT, *parts)

        def near(self, *parts):
            wait_in(ACROSS_INNER, *parts)
            self.plan.run(y, parts, put(rq, rq))

        def end(self, *parts):
            final(self.plan, yx, parts, rq)

    UNIT = {"cross": "fo", "far": "fi", "far_end": 0, "out": "no", "near": "ni", "end": 1}
    inner_steps = INNER_STEPS
    inner_plan = Plan([UNIT[step[0]] for block in inner_steps for step in block if step[0] in UNIT])
    inner_work = Inner(inner_plan)

    class Outer:
        def __init__(self, plan):
            self.plan = plan

        def sum(self, *parts):
            self.plan.run(y, parts, put(st1))

        def go_sum(self, *parts):
            go(SUM_IN, *parts)

        def go_y(self, *parts):
            go(Y_IN, *parts)

        def go_w(self, g):
            w_inward(g).start()

        def end(self, *parts):
            wait_in(SUM_OUT, *parts)
            final(self.plan, y, parts, r1)

    OUTER_UNIT = {"sum": "fo", "end": "no"}
    outer_steps = OUTER_STEPS
    outer_plan = Plan([OUTER_UNIT[step[0]] for block in outer_steps for step in block if step[0] in OUTER_UNIT])
    outer_work = Outer(outer_plan)

    @pl.when(outer)
    def _():
        w_inward(0).start()
        outer_plan.load(0)

    @pl.when(inner)
    def _():
        inner_plan.load(0)

    for k in range(len(FEATURES)):
        feature(k)

        @pl.when(inner)
        def _():
            for step in inner_steps[k]:
                if step[0] == "plane":
                    relay_plane(step[1])
                elif step[0] == "core":
                    relay_core(step[1])
                else:
                    getattr(inner_work, step[0])(*step[1:])
            if k == len(FEATURES) - 1:
                settle()
                for part in range(len(PARTS)):
                    moving(ACROSS_OUTER, part).wait_send()
                    moving(ACROSS_INNER, part).wait_send()
                    moving(SUM_OUT, part).wait_send()
                for g in range(2):
                    for i in range(3):
                        w_plane(g, i).wait_send()
                    for i in range(4):
                        w_core(g, i).wait_send()

        @pl.when(outer)
        def _():
            for step in outer_steps[k]:
                getattr(outer_work, step[0])(*step[1:])
            if k == len(FEATURES) - 1:
                settle()
                for part in range(len(PARTS)):
                    moving(SUM_IN, part).wait_send()
                    moving(Y_IN, part).wait_send()
                for g in range(2):
                    w_inward(g).wait_send()

    pl.when(s < 7)(rim_copy.wait_send)


INNER_STEPS = (
    (),
    (("plane", 0), ("cross", 0)),
    (("cross", 1),),
    (("core", 0), ("cross", 2), ("far", 0, 1), ("far_end", 0, 1), ("out", 0, 1)),
    (
        ("cross", 3), ("out", 2), ("plane", 1), ("cross", 4), ("out", 3), ("far", 2), ("core", 1), ("cross", 5),
        ("far_end", 2), ("out", 4, 5), ("near", 0, 1), ("end", 0, 1), ("far", 3), ("far_end", 3), ("near", 2), ("end", 2),
        ("far", 4, 5), ("far_end", 4), ("near", 3), ("end", 3), ("far_end", 5), ("near", 4, 5), ("end", 4, 5),
    ),
)
OUTER_STEPS = (
    (("sum", 0), ("go_sum", 0)),
    (("sum", 1), ("go_sum", 1), ("go_y", 0, 1)),
    (("sum", 2), ("go_sum", 2)),
    (("sum", 3), ("go_sum", 3), ("go_w", 1)),
    (
        ("sum", 4, 5), ("go_sum", 4), ("go_y", 2), ("go_sum", 5), ("go_y", 3, 4, 5),
        ("end", 0, 1), ("end", 2), ("end", 3), ("end", 4, 5),
    ),
)


def lined(qkv, short_taps, medium_taps, skip_gain, w_out, resid, steer):
    channels, slab = qkv.shape[1:]
    width = resid.shape[0]
    short = jnp.swapaxes(short_taps.astype(F32), 1, 2)
    medium = medium_taps.astype(F32)
    medium = jnp.concatenate([medium[:, :1] + skip_gain[:, None], medium[:, 1:]], 1).T
    whole = pl.BlockSpec(memory_space=pltpu.VMEM)
    anywhere = pl.BlockSpec(memory_space=pl.ANY)
    token = lambda: pltpu.VMEM((slab, channels), BF16)
    dma = pltpu.SemaphoreType.DMA
    span = 512
    return pl.pallas_call(
        line_kernel,
        in_specs=[anywhere] * 3 + [whole] * 3,
        out_specs=[anywhere] * 4,
        out_shape=[
            jax.ShapeDtypeStruct(resid.shape, BF16),
            jax.ShapeDtypeStruct((channels, width), BF16),
            jax.ShapeDtypeStruct((channels, width), BF16),
            jax.ShapeDtypeStruct((3, channels, 256), BF16),
        ],
        scratch_shapes=[token() for _ in range(8)]
        + [
            pltpu.VMEM((2, width // COLS, channels, COLS), BF16),
            pltpu.VMEM((2, 3, LANES, span), BF16),
            pltpu.VMEM((2, width, 256), BF16),
            pltpu.VMEM((3, span, LANES), F32),
            pltpu.VMEM((span - LANES, LANES), F32),
            pltpu.VMEM((9, EDGE + (span - LANES) // 4, LANES), F32),
            pltpu.VMEM((EDGE + 64, LANES), F32),
            pltpu.VMEM((256, LANES), F32),
            dma((5, len(PARTS))),
            dma((5, len(PARTS))),
            dma((2, 8)),
            dma((2, 8)),
            dma,
            dma,
            dma((2, width // COLS)),
            dma((2, 2)),
            dma((2, 2)),
        ],
        compiler_params=pltpu.CompilerParams(
            collective_id=0, has_side_effects=True, vmem_limit_bytes=VMEM_LIMIT
        ),
        cost_estimate=pl.CostEstimate(
            flops=12 * channels * slab * width, bytes_accessed=20 * channels * width, transcendentals=0
        ),
    )(qkv, w_out, resid, short, nine_taps(medium), steer[None])[0]


def solution(mesh):
    line = mesh.shape["mp"] == 4 and mesh.shape["seq"] == 8
    return jax.shard_map(
        lined if line else shards,
        mesh=mesh,
        in_specs=(
            P(None, "mp", "seq"),
            P(None, "mp", None),
            P("mp", None),
            P("mp"),
            P("mp", None),
            P("mp", "seq"),
            P("mp"),
        ),
        out_specs=P("mp", "seq"),
        check_vma=False,
    )
```

```python
import functools

import jax
import jax.numpy as jnp
from jax import lax
from jax.experimental import pallas as pl
from jax.experimental.pallas import tpu as pltpu
from jax.sharding import PartitionSpec as P

STAPS = 7
MTAPS = 128
LANES = 128
F32 = jnp.float32
BF16 = jnp.bfloat16
MESH = pl.DeviceIdType.MESH


def from_behind(value, axis, steps):
    count = lax.axis_size(axis)
    return lax.ppermute(value, axis, [(source, source + steps) for source in range(count - steps)])


def chunks(slab):
    sizes = [1]
    left = slab // LANES - 3
    while left > 0:
        sizes.append(min(left, 2 if len(sizes) == 1 else 3))
        left -= sizes[-1]
    sizes.append(2)
    plan, end = [], slab
    for size in sizes:
        end -= size * LANES
        plan.append((end, size * LANES))
    return plan


def feature_kernel(blocks, *refs):
    token_refs = refs[:blocks]
    short_ref, medium_ref, y_ref, wide, kv = refs[blocks:]
    for at, ref in enumerate(token_refs):
        for s in range(3):
            if s > 0 or at > 0:
                wide[s, at * LANES : (at + 1) * LANES] = ref[s].astype(F32).T

    def short(s, row):
        total = short_ref[s, 0:1] * wide[s, row : row + LANES]
        for j in range(1, STAPS):
            total = total + short_ref[s, j : j + 1] * wide[s, row - j : row - j + LANES]
        return total

    for at in range(1, blocks):
        row = at * LANES
        kv[row - LANES : row] = (short(1, row) * short(2, row)).astype(BF16).astype(F32)

    for at in range(blocks - 2):
        row = at * LANES
        total = jnp.zeros((LANES, LANES), F32)
        for low in range(8):
            start = row + 8 - low
            block = kv[start : start + LANES + MTAPS - 8]
            for high in range(0, MTAPS, 8):
                first = MTAPS - 8 - high
                total = total + medium_ref[high + low : high + low + 1] * block[first : first + LANES]
        y_ref[row : row + LANES] = (short(0, row + 2 * LANES) * total).astype(BF16)


def features(sources, short, medium):
    channels = short.shape[2]
    blocks = len(sources)
    tokens = (blocks - 2) * LANES
    return pl.pallas_call(
        functools.partial(feature_kernel, blocks),
        grid=(channels // LANES,),
        in_specs=[pl.BlockSpec((3, LANES, LANES), lambda c, at=at: (0, c, at)) for _, at in sources]
        + [
            pl.BlockSpec((3, STAPS, LANES), lambda c: (0, 0, c)),
            pl.BlockSpec((MTAPS, LANES), lambda c: (0, c)),
        ],
        out_specs=pl.BlockSpec((tokens, LANES), lambda c: (0, c)),
        out_shape=jax.ShapeDtypeStruct((tokens, channels), BF16),
        scratch_shapes=[
            pltpu.VMEM((3, blocks * LANES, LANES), F32),
            pltpu.VMEM(((blocks - 1) * LANES, LANES), F32),
        ],
        cost_estimate=pl.CostEstimate(
            flops=2 * channels * tokens * (MTAPS + 4 * STAPS),
            bytes_accessed=6 * channels * blocks * LANES,
            transcendentals=0,
        ),
    )(*[array for array, _ in sources], short, medium)


def finish_kernel(*refs):
    resid_ref, steer_ref, proj_ref, out_ref = refs[0], refs[1], refs[2], refs[-1]
    gain = proj_ref[...].astype(F32) + steer_ref[...]
    out_ref[...] = (resid_ref[...].astype(F32) + gain.T).astype(BF16)


def finish(resid, steer, proj, out, first):
    tokens, channels = proj.shape
    rows = min(channels, 1024)
    at = first // LANES
    column = pl.BlockSpec((rows, LANES), lambda t, c: (c, at + t))
    specs = [
        column,
        pl.BlockSpec((1, rows), lambda t, c: (0, c)),
        pl.BlockSpec((LANES, rows), lambda t, c: (t, c)),
    ]
    held = [] if out is None else [out]
    return pl.pallas_call(
        finish_kernel,
        grid=(tokens // LANES, channels // rows),
        in_specs=specs + [pl.BlockSpec(memory_space=pl.ANY)] * len(held),
        out_specs=column,
        out_shape=jax.ShapeDtypeStruct(resid.shape, BF16),
        input_output_aliases={3: 0} if held else {},
        cost_estimate=pl.CostEstimate(
            flops=2 * channels * tokens, bytes_accessed=6 * channels * tokens, transcendentals=0
        ),
    )(resid, steer, proj, *held)


def shards(qkv, short_taps, medium_taps, skip_gain, w_out, resid, steer):
    slab = qkv.shape[2]
    short = jnp.swapaxes(short_taps.astype(F32), 1, 2)
    medium = medium_taps.astype(F32)
    medium = jnp.concatenate([medium[:, :1] + skip_gain[:, None], medium[:, 1:]], 1).T
    rim = from_behind(qkv[:, :, slab - 2 * LANES :], "seq", 1)
    out = None
    projs = []
    for first, tokens in chunks(slab):
        at = first // LANES
        sources = [(rim, i + 2) if i < 0 else (qkv, i) for i in range(at - 2, at + tokens // LANES)]
        y = features(sources, short, medium)
        part = jnp.dot(y, w_out, preferred_element_type=F32).astype(BF16)
        proj = lax.psum_scatter(part, "mp", scatter_dimension=1, tiled=True)
        projs.append((first, proj))
    for first, proj in projs:
        out = finish(resid, steer[None], proj, out, first)
    return out


PHASE = MTAPS // 4
EDGE = 8
COLS = 512
VMEM_LIMIT = 62 << 20
FEATURES = ((896, 128), (768, 128), (512, 256), (256, 256), (0, 256))
PARTS = ((896, 128), (768, 128), (512, 256), (256, 256), (128, 128), (64, 64), (0, 64))
PLANE = (2, 4, 6)
SUM_IN, Y_IN, ACROSS_OUTER, ACROSS_INNER, SUM_OUT = range(5)


def split_taps(c, lanes, medium_ref, skip_ref, nine, spare):
    spare[0:MTAPS] = medium_ref[pl.ds(pl.multiple_of(c * LANES, LANES), LANES)].astype(F32).T
    spare[0:1] = spare[0:1] + skip_ref[0:1, lanes]
    phase = [spare[pl.ds(p, PHASE, stride=4)] for p in range(4)]
    even = [phase[0], phase[2], phase[0] + phase[2]]
    odd = [phase[1], phase[3], phase[1] + phase[3]]
    for i, x in enumerate(even + odd + [a + b for a, b in zip(even, odd)]):
        nine[i * PHASE : (i + 1) * PHASE, lanes] = x


def filtered(blocks, known, kept, short_ref, nine_ref, top, lanes, wide, kv, xs, back, med):
    count = (blocks - 2) * LANES // 4
    held = (blocks - 1) * LANES // 4

    def short(s, row):
        total = short_ref[s, 0:1, lanes] * wide[s, row : row + LANES]
        for j in range(1, STAPS):
            total = total + short_ref[s, j : j + 1, lanes] * wide[s, row - j : row - j + LANES]
        return total

    for at in range(1, blocks - 1 if known else blocks):
        row = at * LANES
        kv[row - LANES : row] = (short(1, row) * short(2, row)).astype(BF16).astype(F32)
    if known:
        kv[(blocks - 2) * LANES : (blocks - 1) * LANES] = top[:, lanes]
    if kept:
        top[:, lanes] = kv[0:LANES]
    phase = [kv[pl.ds(p, held, stride=4)] for p in range(4)]
    even = [phase[0], phase[2], phase[0] + phase[2]]
    odd = [phase[1], phase[3], phase[1] + phase[3]]
    for i, x in enumerate(even + odd + [a + b for a, b in zip(even, odd)]):
        xs[i, EDGE : EDGE + held] = x

    def conv(i, edge):
        size, total = count + edge, None
        for low in range(8):
            start = EDGE + 8 - edge - low
            block = xs[i, start : start + size + PHASE - 8]
            for high in range(0, PHASE, 8):
                first = PHASE - 8 - high
                tap = i * PHASE + high + low
                term = nine_ref[tap : tap + 1, lanes] * block[first : first + size]
                total = term if total is None else total + term
        return total

    def delayed(value):
        back[0 : count + EDGE] = value
        return back[EDGE - 1 : EDGE - 1 + count]

    def pair(g, edge):
        first, second, both = conv(3 * g, edge), conv(3 * g + 1, EDGE), conv(3 * g + 2, edge)
        return first[edge:] + delayed(second), both - first - second[EDGE - edge :]

    odd0, odd1 = pair(1, EDGE)
    late, odd1 = delayed(odd1), odd1[EDGE:]
    even0, even1 = pair(0, 0)
    both0, both1 = pair(2, 0)
    med[pl.ds(0, count, stride=4)] = even0 + late
    med[pl.ds(1, count, stride=4)] = both0 - even0 - odd0
    med[pl.ds(2, count, stride=4)] = even1 + odd0
    med[pl.ds(3, count, stride=4)] = both1 - even1 - odd1
    for at in range(blocks - 2):
        row = at * LANES
        yield row, (short(0, row + 2 * LANES) * med[row : row + LANES]).astype(BF16)


def line_kernel(
    qkv, w_out, resid, short_taps, medium_ref, skip_ref, steer_ref,
    out, wx_far, wx_near, rim,
    y, yx, st1, st2, st3, r1, rp, rq, wbuf, qbuf, rbuf, short_ref, nine_ref, top, wide, kv, xs, back, med,
    send, recv, w_send, w_recv, rim_send, rim_recv, fetch_sem, q_sem, r_sem,
):
    s, m = lax.axis_index("seq"), lax.axis_index("mp")
    channels, slab = qkv.shape[1], qkv.shape[2]
    width = resid.shape[0]
    steps = width // COLS
    low = m < 2
    inner = jnp.logical_or(m == 1, m == 2)
    outer = jnp.logical_not(inner)
    far_outer, far_inner = jnp.where(low, 3, 0), jnp.where(low, 2, 1)
    near_inner, near_outer = jnp.where(low, 1, 2), jnp.where(low, 0, 3)
    inward = (s, near_inner)
    outward = (s, near_outer)
    opposite = (s, jnp.where(low, 2, 1))

    barrier = pltpu.get_barrier_semaphore()

    def greet(condition, device):
        @pl.when(condition)
        def _():
            pl.semaphore_signal(barrier, inc=1, device_id=device, device_id_type=MESH)

    greet(m < 3, (s, jnp.minimum(m + 1, 3)))
    greet(m > 0, (s, jnp.maximum(m - 1, 0)))
    greet(s < 7, (jnp.minimum(s + 1, 7), m))
    greet(s > 0, (jnp.maximum(s - 1, 0), m))
    for flip in (1, *PLANE):
        pl.semaphore_signal(barrier, inc=1, device_id=(s ^ flip, m), device_id_type=MESH)
    one = lambda c: jnp.where(c, 1, 0)
    pl.semaphore_wait(barrier, 4 + one(m < 3) + one(m > 0) + one(s < 7) + one(s > 0))

    def remote(src, dst, sent, got, device):
        return pltpu.make_async_remote_copy(
            src_ref=src, dst_ref=dst, send_sem=sent, recv_sem=got, device_id=device, device_id_type=MESH
        )

    rim_copy = remote(qkv.at[:, :, slab - 256 : slab], rim, rim_send, rim_recv, (jnp.minimum(s + 1, 7), m))
    pl.when(s < 7)(rim_copy.start)

    share = channels // 16
    held = (wx_far, wx_near)

    def rows_of(device, h):
        return pl.ds(pl.multiple_of((device * 2 + h) * share, share), share)

    def w_inward(g, h):
        group = (far_inner, near_inner)[g]
        columns = pl.ds(pl.multiple_of(group * width, width), width)
        return remote(
            w_out.at[rows_of(s, h), columns], held[g].at[rows_of(s, h)], w_send.at[g, h, 0], w_recv.at[g, h, 0], inward
        )

    def w_plane(g, h, i):
        mine = held[g].at[rows_of(s, h)]
        return remote(mine, mine, w_send.at[g, h, 1 + i], w_recv.at[g, h, 1 + i], (s ^ PLANE[i], m))

    def w_core(g, h, i):
        piece = held[g].at[rows_of(s if i == 0 else s ^ PLANE[i - 1], h)]
        return remote(piece, piece, w_send.at[g, h, 4 + i], w_recv.at[g, h, 4 + i], (s ^ 1, m))

    def relay_plane(g, h):
        w_inward(g, h).wait_recv()
        for i in range(3):
            w_plane(g, h, i).start()
        w_core(g, h, 0).start()

    def relay_core(g, h):
        for i in range(3):
            w_plane(g, h, i).wait_recv()
            w_core(g, h, 1 + i).start()

    def relay_end(g):
        for h in range(2):
            for i in range(4):
                w_core(g, h, i).wait_recv()

    def rows(k):
        return pl.ds(PARTS[k][0], PARTS[k][1])

    def moving(kind, k):
        src, dst, device = {
            SUM_IN: (st1, r1, inward),
            Y_IN: (y, yx, inward),
            ACROSS_OUTER: (st1, rp, opposite),
            ACROSS_INNER: (st2, rq, opposite),
            SUM_OUT: (st3, r1, outward),
        }[kind]
        return remote(src.at[rows(k)], dst.at[rows(k)], send.at[kind, k], recv.at[kind, k], device)

    def fetch(which, half, j):
        if which in (0, 1):
            block = held[which].at[:, pl.ds(pl.multiple_of(j * COLS, COLS), COLS)]
        else:
            group = {"fo": far_outer, "fi": far_inner, "ni": near_inner, "no": near_outer}[which]
            block = w_out.at[:, pl.ds(pl.multiple_of(group * width + j * COLS, COLS), COLS)]
        return pltpu.make_async_copy(block, wbuf.at[half, j], fetch_sem.at[half, j])

    class Plan:
        def __init__(self, units):
            self.units, self.at, self.ended = units, 0, set()

        def load(self, i):
            if i < len(self.units):
                which = self.units[i]
                if which in (0, 1) and which not in self.ended:
                    self.ended.add(which)
                    relay_end(which)
                for j in range(steps):
                    fetch(which, i % 2, j).start()

        def run(self, src, parts, each):
            i = self.at
            self.at += 1
            self.load(i + 1)
            first = PARTS[parts[-1]][0]
            tokens = sum(PARTS[k][1] for k in parts)

            def body(j, carry):
                fetch(self.units[i], i % 2, j).wait()
                total = jnp.dot(src[first : first + tokens], wbuf[i % 2, j], preferred_element_type=F32)
                each(total, j, pl.ds(first, tokens), pl.ds(pl.multiple_of(j * COLS, COLS), COLS))
                return carry

            lax.fori_loop(0, steps, body, 0)

    def put(dst, *adds):
        def each(total, j, at, columns):
            for ref in adds:
                total = total + ref[at, columns].astype(F32)
            dst[at, columns] = total.astype(BF16)

        return each

    def resid_in(slot, first, tokens):
        return pltpu.make_async_copy(
            resid.at[:, first : first + tokens], rbuf.at[slot, :, 0:tokens], r_sem.at[0, slot]
        )

    def out_of(slot, first, tokens):
        return pltpu.make_async_copy(
            rbuf.at[slot, :, 0:tokens], out.at[:, first : first + tokens], r_sem.at[1, slot]
        )

    leaving = []

    def final(kind, parts, left, right):
        first = PARTS[parts[-1]][0]
        tokens = sum(PARTS[k][1] for k in parts)
        slot = len(leaving) % 2
        if len(leaving) >= 2:
            out_of(*leaving[-2]).wait()
        resid_in(slot, first, tokens).start()
        leaving.append((slot, first, tokens))
        wait_in(kind, *parts)
        resid_in(slot, first, tokens).wait()
        at = pl.ds(first, tokens)

        def body(j, carry):
            columns = pl.ds(pl.multiple_of(j * COLS, COLS), COLS)
            total = left[at, columns].astype(F32) + right[at, columns].astype(F32) + steer_ref[0:1, columns]
            rbuf[slot, columns, 0:tokens] = (rbuf[slot, columns, 0:tokens].astype(F32) + total.T).astype(BF16)
            return carry

        lax.fori_loop(0, steps, body, 0)
        out_of(slot, first, tokens).start()

    def settle():
        for left in leaving[-2:]:
            out_of(*left).wait()
        leaving.clear()

    blocks_of_channels = channels // LANES

    def load(k, c, slot, act):
        first, tokens = FEATURES[k]
        span = tokens + 256
        lanes = pl.ds(pl.multiple_of(c * LANES, LANES), LANES)
        if first > 0:
            act(pltpu.make_async_copy(
                qkv.at[:, lanes, first - 256 : first + tokens], qbuf.at[slot, :, :, 0:span], q_sem.at[0, slot]
            ))
        else:
            act(pltpu.make_async_copy(
                qkv.at[:, lanes, 0:tokens], qbuf.at[slot, :, :, 256:span], q_sem.at[0, slot]
            ))

            @pl.when(s > 0)
            def _():
                act(pltpu.make_async_copy(rim.at[:, lanes], qbuf.at[slot, :, :, 0:256], q_sem.at[1, slot]))

    def begin(k):
        if FEATURES[k][0] == 0:

            @pl.when(s > 0)
            def _():
                rim_copy.wait_recv()

            @pl.when(s == 0)
            def _():
                qbuf[:, :, :, 0:256] = jnp.zeros((2, 3, LANES, 256), BF16)

        load(k, 0, 0, lambda copy: copy.start())

    def feature(k, start, stop):
        first, tokens = FEATURES[k]
        blocks = (tokens + 256) // LANES
        known, kept = k > 0, k + 1 < len(FEATURES)

        def body(c, carry):
            slot = lax.rem(c, 2)

            @pl.when(c + 1 < blocks_of_channels)
            def _():
                load(k, c + 1, 1 - slot, lambda copy: copy.start())

            load(k, c, slot, lambda copy: copy.wait())
            lanes = pl.ds(pl.multiple_of(c * LANES, LANES), LANES)
            if k == 0:
                split_taps(c, lanes, medium_ref, skip_ref, nine_ref, med)
            for at in range(blocks):
                for i in range(3):
                    if at > 0 if i == 0 else not (known and at == blocks - 1):
                        wide[i, at * LANES : (at + 1) * LANES] = (
                            qbuf[slot, i, :, at * LANES : (at + 1) * LANES].astype(F32).T
                        )
            pieces = filtered(
                blocks, known, kept, short_ref, nine_ref, top, lanes, wide, kv, xs, back, med
            )
            for row, value in pieces:
                y[first + row : first + row + LANES, lanes] = value
            return carry

        lax.fori_loop(start, stop, body, 0)
        if stop == blocks_of_channels and k + 1 < len(FEATURES):
            begin(k + 1)

    def wait_in(kind, *parts):
        for k in parts:
            moving(kind, k).wait_recv()

    def go(kind, *parts):
        for k in parts:
            moving(kind, k).start()

    class Inner:
        def __init__(self, plan):
            self.plan = plan

        def cross(self, *parts):
            wait_in(SUM_IN, *parts)
            self.plan.run(y, parts, put(st1, r1))
            go(ACROSS_OUTER, *parts)

        def far(self, *parts):
            self.plan.run(y, parts, put(st2))

        def far_end(self, *parts):
            wait_in(Y_IN, *parts)
            self.plan.run(yx, parts, put(st2, st2))
            go(ACROSS_INNER, *parts)

        def out(self, *parts):
            wait_in(ACROSS_OUTER, *parts)
            self.plan.run(y, parts, put(st3, rp))
            go(SUM_OUT, *parts)

        def near(self, *parts):
            self.plan.run(y, parts, put(r1))

        def near_end(self, *parts):
            self.plan.run(yx, parts, put(r1, r1))

        def final(self, *parts):
            final(ACROSS_INNER, parts, r1, rq)

    UNIT = {"cross": "fo", "far": "fi", "far_end": 0, "out": "no", "near": "ni", "near_end": 1}
    inner_plan = Plan([UNIT[step[0]] for entry in SCHEDULE for step in entry[3] if step[0] in UNIT])
    inner_work = Inner(inner_plan)

    class Outer:
        def __init__(self, plan):
            self.plan = plan

        def sum(self, *parts):
            self.plan.run(y, parts, put(st1))

        def go_sum(self, *parts):
            go(SUM_IN, *parts)

        def go_y(self, *parts):
            go(Y_IN, *parts)

        def go_w(self, g):
            for h in range(2):
                w_inward(g, h).start()

        def out(self, *parts):
            self.plan.run(y, parts, put(rp))

        def final(self, *parts):
            final(SUM_OUT, parts, rp, r1)

    OUTER_UNIT = {"sum": "fo", "out": "no"}
    outer_plan = Plan([OUTER_UNIT[step[0]] for entry in SCHEDULE for step in entry[4] if step[0] in OUTER_UNIT])
    outer_work = Outer(outer_plan)

    begin(0)

    @pl.when(outer)
    def _():
        for h in range(2):
            w_inward(0, h).start()
        outer_plan.load(0)

    @pl.when(inner)
    def _():
        inner_plan.load(0)

    short_ref[...] = short_taps[...].astype(F32)
    for number, (k, start, stop, inner_steps, outer_steps) in enumerate(SCHEDULE):
        feature(k, start, stop)
        ending = number == len(SCHEDULE) - 1

        @pl.when(inner)
        def _():
            for step in inner_steps:
                if step[0] == "plane":
                    relay_plane(*step[1:])
                elif step[0] == "core":
                    relay_core(*step[1:])
                else:
                    getattr(inner_work, step[0])(*step[1:])
            if ending:
                settle()
                for part in range(len(PARTS)):
                    moving(ACROSS_OUTER, part).wait_send()
                    moving(ACROSS_INNER, part).wait_send()
                    moving(SUM_OUT, part).wait_send()
                for g in range(2):
                    for h in range(2):
                        for i in range(3):
                            w_plane(g, h, i).wait_send()
                        for i in range(4):
                            w_core(g, h, i).wait_send()

        @pl.when(outer)
        def _():
            for step in outer_steps:
                getattr(outer_work, step[0])(*step[1:])
            if ending:
                settle()
                for part in range(len(PARTS)):
                    moving(SUM_IN, part).wait_send()
                    moving(Y_IN, part).wait_send()
                for g in range(2):
                    for h in range(2):
                        w_inward(g, h).wait_send()

    pl.when(s < 7)(rim_copy.wait_send)


SCHEDULE = (
    (0, 0, 11, (("plane", 0, 0),), ()),
    (0, 11, 16, (), (("sum", 0), ("go_sum", 0))),
    (1, 0, 8, (("plane", 0, 1),), ()),
    (1, 8, 16, (), (("sum", 1), ("go_sum", 1), ("go_y", 0, 1))),
    (2, 0, 4, (("cross", 0),), ()),
    (2, 4, 11, (("core", 0, 0), ("cross", 1)), ()),
    (2, 11, 16, (("core", 0, 1), ("far", 0, 1), ("far_end", 0)), (("sum", 2), ("go_sum", 2))),
    (3, 0, 8, (("far_end", 1), ("out", 0, 1)), ()),
    (3, 8, 16, (("cross", 2),), (("sum", 3), ("go_sum", 3))),
    (4, 0, 14, (("cross", 3),), ()),
    (4, 14, 16, (
        ("near", 0, 1), ("out", 2), ("near", 2), ("plane", 1, 0), ("cross", 4), ("plane", 1, 1),
        ("far", 2), ("far_end", 2), ("core", 1, 0), ("cross", 5), ("cross", 6), ("core", 1, 1), ("out", 3), ("near", 3),
        ("far", 3), ("far_end", 3), ("out", 4, 5, 6), ("far", 4, 5, 6), ("far_end", 4), ("near", 4, 5, 6), ("far_end", 5), ("near_end", 0, 1), ("far_end", 6),
        ("near_end", 2), ("near_end", 3), ("near_end", 4, 5, 6), ("final", 0, 1), ("final", 2),
        ("final", 3), ("final", 4), ("final", 5, 6),
    ), (
        ("sum", 4, 5, 6), ("go_sum", 4), ("go_w", 1), ("go_y", 2), ("go_sum", 5, 6), ("go_y", 3, 4, 5, 6),
        ("out", 0, 1), ("out", 2), ("out", 3), ("out", 4, 5, 6),
        ("final", 0, 1), ("final", 2), ("final", 3), ("final", 4, 5, 6),
    )),
)


def lined(qkv, short_taps, medium_taps, skip_gain, w_out, resid, steer):
    channels, slab = qkv.shape[1:]
    width = resid.shape[0]
    whole = pl.BlockSpec(memory_space=pltpu.VMEM)
    anywhere = pl.BlockSpec(memory_space=pl.ANY)
    token = lambda: pltpu.VMEM((slab, channels), BF16)
    dma = pltpu.SemaphoreType.DMA
    span = 512
    return pl.pallas_call(
        line_kernel,
        in_specs=[anywhere] * 3 + [whole] * 4,
        out_specs=[anywhere] * 4,
        out_shape=[
            jax.ShapeDtypeStruct(resid.shape, BF16),
            jax.ShapeDtypeStruct((channels, width), BF16),
            jax.ShapeDtypeStruct((channels, width), BF16),
            jax.ShapeDtypeStruct((3, channels, 256), BF16),
        ],
        scratch_shapes=[token() for _ in range(8)]
        + [
            pltpu.VMEM((2, width // COLS, channels, COLS), BF16),
            pltpu.VMEM((2, 3, LANES, span), BF16),
            pltpu.VMEM((2, width, 256), BF16),
            pltpu.VMEM((3, STAPS, channels), F32),
            pltpu.VMEM((9 * PHASE, channels), F32),
            pltpu.VMEM((LANES, channels), F32),
            pltpu.VMEM((3, span, LANES), F32),
            pltpu.VMEM((span - LANES, LANES), F32),
            pltpu.VMEM((9, EDGE + (span - LANES) // 4, LANES), F32),
            pltpu.VMEM((EDGE + 64, LANES), F32),
            pltpu.VMEM((256, LANES), F32),
            dma((5, len(PARTS))),
            dma((5, len(PARTS))),
            dma((2, 2, 8)),
            dma((2, 2, 8)),
            dma,
            dma,
            dma((2, width // COLS)),
            dma((2, 2)),
            dma((2, 2)),
        ],
        compiler_params=pltpu.CompilerParams(
            collective_id=0, has_side_effects=True, vmem_limit_bytes=VMEM_LIMIT
        ),
        cost_estimate=pl.CostEstimate(
            flops=12 * channels * slab * width, bytes_accessed=20 * channels * width, transcendentals=0
        ),
    )(qkv, w_out, resid, jnp.swapaxes(short_taps, 1, 2), medium_taps, skip_gain[None], steer[None])[0]


def solution(mesh):
    line = mesh.shape["mp"] == 4 and mesh.shape["seq"] == 8
    return jax.shard_map(
        lined if line else shards,
        mesh=mesh,
        in_specs=(
            P(None, "mp", "seq"),
            P(None, "mp", None),
            P("mp", None),
            P("mp"),
            P("mp", None),
            P("mp", "seq"),
            P("mp"),
        ),
        out_specs=P("mp", "seq"),
        check_vma=False,
    )
```

```python
import functools

import jax
import jax.numpy as jnp
from jax import lax
from jax.experimental import pallas as pl
from jax.experimental.pallas import tpu as pltpu
from jax.sharding import PartitionSpec as P

STAPS = 7
MTAPS = 128
LANES = 128
F32 = jnp.float32
BF16 = jnp.bfloat16
MESH = pl.DeviceIdType.MESH


def from_behind(value, axis, steps):
    count = lax.axis_size(axis)
    return lax.ppermute(value, axis, [(source, source + steps) for source in range(count - steps)])


def chunks(slab):
    sizes = [1]
    left = slab // LANES - 3
    while left > 0:
        sizes.append(min(left, 2 if len(sizes) == 1 else 3))
        left -= sizes[-1]
    sizes.append(2)
    plan, end = [], slab
    for size in sizes:
        end -= size * LANES
        plan.append((end, size * LANES))
    return plan


def feature_kernel(blocks, *refs):
    token_refs = refs[:blocks]
    short_ref, medium_ref, y_ref, wide, kv = refs[blocks:]
    for at, ref in enumerate(token_refs):
        for s in range(3):
            if s > 0 or at > 0:
                wide[s, at * LANES : (at + 1) * LANES] = ref[s].astype(F32).T

    def short(s, row):
        total = short_ref[s, 0:1] * wide[s, row : row + LANES]
        for j in range(1, STAPS):
            total = total + short_ref[s, j : j + 1] * wide[s, row - j : row - j + LANES]
        return total

    for at in range(1, blocks):
        row = at * LANES
        kv[row - LANES : row] = (short(1, row) * short(2, row)).astype(BF16).astype(F32)

    for at in range(blocks - 2):
        row = at * LANES
        total = jnp.zeros((LANES, LANES), F32)
        for low in range(8):
            start = row + 8 - low
            block = kv[start : start + LANES + MTAPS - 8]
            for high in range(0, MTAPS, 8):
                first = MTAPS - 8 - high
                total = total + medium_ref[high + low : high + low + 1] * block[first : first + LANES]
        y_ref[row : row + LANES] = (short(0, row + 2 * LANES) * total).astype(BF16)


def features(sources, short, medium):
    channels = short.shape[2]
    blocks = len(sources)
    tokens = (blocks - 2) * LANES
    return pl.pallas_call(
        functools.partial(feature_kernel, blocks),
        grid=(channels // LANES,),
        in_specs=[pl.BlockSpec((3, LANES, LANES), lambda c, at=at: (0, c, at)) for _, at in sources]
        + [
            pl.BlockSpec((3, STAPS, LANES), lambda c: (0, 0, c)),
            pl.BlockSpec((MTAPS, LANES), lambda c: (0, c)),
        ],
        out_specs=pl.BlockSpec((tokens, LANES), lambda c: (0, c)),
        out_shape=jax.ShapeDtypeStruct((tokens, channels), BF16),
        scratch_shapes=[
            pltpu.VMEM((3, blocks * LANES, LANES), F32),
            pltpu.VMEM(((blocks - 1) * LANES, LANES), F32),
        ],
        cost_estimate=pl.CostEstimate(
            flops=2 * channels * tokens * (MTAPS + 4 * STAPS),
            bytes_accessed=6 * channels * blocks * LANES,
            transcendentals=0,
        ),
    )(*[array for array, _ in sources], short, medium)


def finish_kernel(*refs):
    resid_ref, steer_ref, proj_ref, out_ref = refs[0], refs[1], refs[2], refs[-1]
    gain = proj_ref[...].astype(F32) + steer_ref[...]
    out_ref[...] = (resid_ref[...].astype(F32) + gain.T).astype(BF16)


def finish(resid, steer, proj, out, first):
    tokens, channels = proj.shape
    rows = min(channels, 1024)
    at = first // LANES
    column = pl.BlockSpec((rows, LANES), lambda t, c: (c, at + t))
    specs = [
        column,
        pl.BlockSpec((1, rows), lambda t, c: (0, c)),
        pl.BlockSpec((LANES, rows), lambda t, c: (t, c)),
    ]
    held = [] if out is None else [out]
    return pl.pallas_call(
        finish_kernel,
        grid=(tokens // LANES, channels // rows),
        in_specs=specs + [pl.BlockSpec(memory_space=pl.ANY)] * len(held),
        out_specs=column,
        out_shape=jax.ShapeDtypeStruct(resid.shape, BF16),
        input_output_aliases={3: 0} if held else {},
        cost_estimate=pl.CostEstimate(
            flops=2 * channels * tokens, bytes_accessed=6 * channels * tokens, transcendentals=0
        ),
    )(resid, steer, proj, *held)


def shards(qkv, short_taps, medium_taps, skip_gain, w_out, resid, steer):
    slab = qkv.shape[2]
    short = jnp.swapaxes(short_taps.astype(F32), 1, 2)
    medium = medium_taps.astype(F32)
    medium = jnp.concatenate([medium[:, :1] + skip_gain[:, None], medium[:, 1:]], 1).T
    rim = from_behind(qkv[:, :, slab - 2 * LANES :], "seq", 1)
    out = None
    projs = []
    for first, tokens in chunks(slab):
        at = first // LANES
        sources = [(rim, i + 2) if i < 0 else (qkv, i) for i in range(at - 2, at + tokens // LANES)]
        y = features(sources, short, medium)
        part = jnp.dot(y, w_out, preferred_element_type=F32).astype(BF16)
        proj = lax.psum_scatter(part, "mp", scatter_dimension=1, tiled=True)
        projs.append((first, proj))
    for first, proj in projs:
        out = finish(resid, steer[None], proj, out, first)
    return out


PHASE = MTAPS // 4
EDGE = 8
COLS = 512
VMEM_LIMIT = 62 << 20
FEATURES = ((896, 128), (768, 128), (512, 256), (256, 256), (0, 256))
PARTS = (
    (960, 64), (896, 64), (768, 128), (640, 128), (512, 128), (384, 128), (256, 128), (128, 128), (64, 64), (0, 64),
)
PLANE = (2, 4, 6)
SUM_IN, Y_IN, ACROSS_OUTER, ACROSS_INNER, SUM_OUT = range(5)


def split_taps(c, lanes, medium_ref, skip_ref, nine, spare):
    spare[0:MTAPS] = medium_ref[pl.ds(pl.multiple_of(c * LANES, LANES), LANES)].astype(F32).T
    spare[0:1] = spare[0:1] + skip_ref[0:1, lanes]
    phase = [spare[pl.ds(p, PHASE, stride=4)] for p in range(4)]
    even = [phase[0], phase[2], phase[0] + phase[2]]
    odd = [phase[1], phase[3], phase[1] + phase[3]]
    for i, x in enumerate(even + odd + [a + b for a, b in zip(even, odd)]):
        nine[i * PHASE : (i + 1) * PHASE, lanes] = x


def filtered(blocks, known, kept, short_ref, nine_ref, top, lanes, wide, kv, xs, back, med):
    count = (blocks - 2) * LANES // 4
    held = (blocks - 1) * LANES // 4

    def short(s, row):
        total = short_ref[s, 0:1, lanes] * wide[s, row : row + LANES]
        for j in range(1, STAPS):
            total = total + short_ref[s, j : j + 1, lanes] * wide[s, row - j : row - j + LANES]
        return total

    for at in range(1, blocks - 1 if known else blocks):
        row = at * LANES
        kv[row - LANES : row] = (short(1, row) * short(2, row)).astype(BF16).astype(F32)
    if known:
        kv[(blocks - 2) * LANES : (blocks - 1) * LANES] = top[:, lanes]
    if kept:
        top[:, lanes] = kv[0:LANES]
    phase = [kv[pl.ds(p, held, stride=4)] for p in range(4)]
    even = [phase[0], phase[2], phase[0] + phase[2]]
    odd = [phase[1], phase[3], phase[1] + phase[3]]
    for i, x in enumerate(even + odd + [a + b for a, b in zip(even, odd)]):
        xs[i, EDGE : EDGE + held] = x

    def conv(i, edge):
        size, total = count + edge, None
        for low in range(8):
            start = EDGE + 8 - edge - low
            block = xs[i, start : start + size + PHASE - 8]
            for high in range(0, PHASE, 8):
                first = PHASE - 8 - high
                tap = i * PHASE + high + low
                term = nine_ref[tap : tap + 1, lanes] * block[first : first + size]
                total = term if total is None else total + term
        return total

    def delayed(value):
        back[0 : count + EDGE] = value
        return back[EDGE - 1 : EDGE - 1 + count]

    def pair(g, edge):
        first, second, both = conv(3 * g, edge), conv(3 * g + 1, EDGE), conv(3 * g + 2, edge)
        return first[edge:] + delayed(second), both - first - second[EDGE - edge :]

    odd0, odd1 = pair(1, EDGE)
    late, odd1 = delayed(odd1), odd1[EDGE:]
    even0, even1 = pair(0, 0)
    both0, both1 = pair(2, 0)
    med[pl.ds(0, count, stride=4)] = even0 + late
    med[pl.ds(1, count, stride=4)] = both0 - even0 - odd0
    med[pl.ds(2, count, stride=4)] = even1 + odd0
    med[pl.ds(3, count, stride=4)] = both1 - even1 - odd1
    for at in range(blocks - 2):
        row = at * LANES
        yield row, (short(0, row + 2 * LANES) * med[row : row + LANES]).astype(BF16)


def line_kernel(
    qkv, w_out, resid, short_taps, medium_ref, skip_ref, steer_ref,
    out, wx_far, wx_near, rim,
    y, yx, st1, st2, st3, r1, rp, rq, wbuf, qbuf, rbuf, short_ref, nine_ref, top, wide, kv, xs, back, med,
    send, recv, w_send, w_recv, rim_send, rim_recv, fetch_sem, q_sem, r_sem,
):
    s, m = lax.axis_index("seq"), lax.axis_index("mp")
    channels, slab = qkv.shape[1], qkv.shape[2]
    width = resid.shape[0]
    steps = width // COLS
    low = m < 2
    inner = jnp.logical_or(m == 1, m == 2)
    outer = jnp.logical_not(inner)
    far_outer, far_inner = jnp.where(low, 3, 0), jnp.where(low, 2, 1)
    near_inner, near_outer = jnp.where(low, 1, 2), jnp.where(low, 0, 3)
    inward = (s, near_inner)
    outward = (s, near_outer)
    opposite = (s, jnp.where(low, 2, 1))

    barrier = pltpu.get_barrier_semaphore()

    def greet(condition, device):
        @pl.when(condition)
        def _():
            pl.semaphore_signal(barrier, inc=1, device_id=device, device_id_type=MESH)

    greet(m < 3, (s, jnp.minimum(m + 1, 3)))
    greet(m > 0, (s, jnp.maximum(m - 1, 0)))
    greet(s < 7, (jnp.minimum(s + 1, 7), m))
    greet(s > 0, (jnp.maximum(s - 1, 0), m))
    for flip in (1, *PLANE):
        pl.semaphore_signal(barrier, inc=1, device_id=(s ^ flip, m), device_id_type=MESH)
    one = lambda c: jnp.where(c, 1, 0)
    pl.semaphore_wait(barrier, 4 + one(m < 3) + one(m > 0) + one(s < 7) + one(s > 0))

    def remote(src, dst, sent, got, device):
        return pltpu.make_async_remote_copy(
            src_ref=src, dst_ref=dst, send_sem=sent, recv_sem=got, device_id=device, device_id_type=MESH
        )

    rim_copy = remote(qkv.at[:, :, slab - 256 : slab], rim, rim_send, rim_recv, (jnp.minimum(s + 1, 7), m))
    pl.when(s < 7)(rim_copy.start)

    share = channels // 16
    held = (wx_far, wx_near)

    def rows_of(device, h):
        return pl.ds(pl.multiple_of((device * 2 + h) * share, share), share)

    def w_inward(g, h):
        group = (far_inner, near_inner)[g]
        columns = pl.ds(pl.multiple_of(group * width, width), width)
        return remote(
            w_out.at[rows_of(s, h), columns], held[g].at[rows_of(s, h)], w_send.at[g, h, 0], w_recv.at[g, h, 0], inward
        )

    def w_plane(g, h, i):
        mine = held[g].at[rows_of(s, h)]
        return remote(mine, mine, w_send.at[g, h, 1 + i], w_recv.at[g, h, 1 + i], (s ^ PLANE[i], m))

    def w_core(g, h, i):
        piece = held[g].at[rows_of(s if i == 0 else s ^ PLANE[i - 1], h)]
        return remote(piece, piece, w_send.at[g, h, 4 + i], w_recv.at[g, h, 4 + i], (s ^ 1, m))

    def relay_plane(g, h):
        w_inward(g, h).wait_recv()
        for i in range(3):
            w_plane(g, h, i).start()
        w_core(g, h, 0).start()

    def relay_core(g, h):
        for i in range(3):
            w_plane(g, h, i).wait_recv()
            w_core(g, h, 1 + i).start()

    def relay_end(g):
        for h in range(2):
            for i in range(4):
                w_core(g, h, i).wait_recv()

    def rows(k):
        return pl.ds(PARTS[k][0], PARTS[k][1])

    def moving(kind, k):
        src, dst, device = {
            SUM_IN: (st1, r1, inward),
            Y_IN: (y, yx, inward),
            ACROSS_OUTER: (st1, rp, opposite),
            ACROSS_INNER: (st2, rq, opposite),
            SUM_OUT: (st3, r1, outward),
        }[kind]
        return remote(src.at[rows(k)], dst.at[rows(k)], send.at[kind, k], recv.at[kind, k], device)

    def fetch(which, half, j):
        if which in (0, 1):
            block = held[which].at[:, pl.ds(pl.multiple_of(j * COLS, COLS), COLS)]
        else:
            group = {"fo": far_outer, "fi": far_inner, "ni": near_inner, "no": near_outer}[which]
            block = w_out.at[:, pl.ds(pl.multiple_of(group * width + j * COLS, COLS), COLS)]
        return pltpu.make_async_copy(block, wbuf.at[half, j], fetch_sem.at[half, j])

    class Plan:
        def __init__(self, units):
            self.units, self.at, self.ended = units, 0, set()

        def load(self, i):
            if i < len(self.units):
                which = self.units[i]
                if which in (0, 1) and which not in self.ended:
                    self.ended.add(which)
                    relay_end(which)
                for j in range(steps):
                    fetch(which, i % 2, j).start()

        def run(self, src, parts, each):
            i = self.at
            self.at += 1
            self.load(i + 1)
            first = PARTS[parts[-1]][0]
            tokens = sum(PARTS[k][1] for k in parts)

            def body(j, carry):
                fetch(self.units[i], i % 2, j).wait()
                total = jnp.dot(src[first : first + tokens], wbuf[i % 2, j], preferred_element_type=F32)
                each(total, j, pl.ds(first, tokens), pl.ds(pl.multiple_of(j * COLS, COLS), COLS))
                return carry

            lax.fori_loop(0, steps, body, 0)

    def put(dst, *adds):
        def each(total, j, at, columns):
            for ref in adds:
                total = total + ref[at, columns].astype(F32)
            dst[at, columns] = total.astype(BF16)

        return each

    def resid_in(slot, first, tokens):
        return pltpu.make_async_copy(
            resid.at[:, first : first + tokens], rbuf.at[slot, :, 0:tokens], r_sem.at[0, slot]
        )

    def out_of(slot, first, tokens):
        return pltpu.make_async_copy(
            rbuf.at[slot, :, 0:tokens], out.at[:, first : first + tokens], r_sem.at[1, slot]
        )

    leaving = []

    def final(kind, parts, left, right):
        first = PARTS[parts[-1]][0]
        tokens = sum(PARTS[k][1] for k in parts)
        slot = len(leaving) % 2
        if len(leaving) >= 2:
            out_of(*leaving[-2]).wait()
        resid_in(slot, first, tokens).start()
        leaving.append((slot, first, tokens))
        wait_in(kind, *parts)
        resid_in(slot, first, tokens).wait()
        at = pl.ds(first, tokens)

        def body(j, carry):
            columns = pl.ds(pl.multiple_of(j * COLS, COLS), COLS)
            total = left[at, columns].astype(F32) + right[at, columns].astype(F32) + steer_ref[0:1, columns]
            rbuf[slot, columns, 0:tokens] = (rbuf[slot, columns, 0:tokens].astype(F32) + total.T).astype(BF16)
            return carry

        lax.fori_loop(0, steps, body, 0)
        out_of(slot, first, tokens).start()

    def settle():
        for left in leaving[-2:]:
            out_of(*left).wait()
        leaving.clear()

    blocks_of_channels = channels // LANES

    def load(k, c, slot, act):
        first, tokens = FEATURES[k]
        span = tokens + 256
        lanes = pl.ds(pl.multiple_of(c * LANES, LANES), LANES)
        if first > 0:
            act(pltpu.make_async_copy(
                qkv.at[:, lanes, first - 256 : first + tokens], qbuf.at[slot, :, :, 0:span], q_sem.at[0, slot]
            ))
        else:
            act(pltpu.make_async_copy(
                qkv.at[:, lanes, 0:tokens], qbuf.at[slot, :, :, 256:span], q_sem.at[0, slot]
            ))

            @pl.when(s > 0)
            def _():
                act(pltpu.make_async_copy(rim.at[:, lanes], qbuf.at[slot, :, :, 0:256], q_sem.at[1, slot]))

    def begin(k):
        if FEATURES[k][0] == 0:

            @pl.when(s > 0)
            def _():
                rim_copy.wait_recv()

            @pl.when(s == 0)
            def _():
                qbuf[:, :, :, 0:256] = jnp.zeros((2, 3, LANES, 256), BF16)

        load(k, 0, 0, lambda copy: copy.start())

    def feature(k, start, stop):
        first, tokens = FEATURES[k]
        blocks = (tokens + 256) // LANES
        known, kept = k > 0, k + 1 < len(FEATURES)

        def body(c, carry):
            slot = lax.rem(c, 2)

            @pl.when(c + 1 < blocks_of_channels)
            def _():
                load(k, c + 1, 1 - slot, lambda copy: copy.start())

            load(k, c, slot, lambda copy: copy.wait())
            lanes = pl.ds(pl.multiple_of(c * LANES, LANES), LANES)
            if k == 0:
                split_taps(c, lanes, medium_ref, skip_ref, nine_ref, med)
            for at in range(blocks):
                for i in range(3):
                    if at > 0 if i == 0 else not (known and at == blocks - 1):
                        wide[i, at * LANES : (at + 1) * LANES] = (
                            qbuf[slot, i, :, at * LANES : (at + 1) * LANES].astype(F32).T
                        )
            pieces = filtered(
                blocks, known, kept, short_ref, nine_ref, top, lanes, wide, kv, xs, back, med
            )
            for row, value in pieces:
                y[first + row : first + row + LANES, lanes] = value
            return carry

        lax.fori_loop(start, stop, body, 0)
        if stop == blocks_of_channels and k + 1 < len(FEATURES):
            begin(k + 1)

    def wait_in(kind, *parts):
        for k in parts:
            moving(kind, k).wait_recv()

    def go(kind, *parts):
        for k in parts:
            moving(kind, k).start()

    class Inner:
        def __init__(self, plan):
            self.plan = plan

        def cross(self, *parts):
            wait_in(SUM_IN, *parts)
            self.plan.run(y, parts, put(st1, r1))
            go(ACROSS_OUTER, *parts)

        def far(self, *parts):
            self.plan.run(y, parts, put(st2))

        def far_end(self, *parts):
            wait_in(Y_IN, *parts)
            self.plan.run(yx, parts, put(st2, st2))
            go(ACROSS_INNER, *parts)

        def out(self, *parts):
            wait_in(ACROSS_OUTER, *parts)
            self.plan.run(y, parts, put(st3, rp))
            go(SUM_OUT, *parts)

        def near(self, *parts):
            self.plan.run(y, parts, put(r1))

        def near_end(self, *parts):
            self.plan.run(yx, parts, put(r1, r1))

        def final(self, *parts):
            final(ACROSS_INNER, parts, r1, rq)

    UNIT = {"cross": "fo", "far": "fi", "far_end": 0, "out": "no", "near": "ni", "near_end": 1}
    inner_plan = Plan([UNIT[step[0]] for entry in SCHEDULE for step in entry[3] if step[0] in UNIT])
    inner_work = Inner(inner_plan)

    class Outer:
        def __init__(self, plan):
            self.plan = plan

        def sum(self, *parts):
            self.plan.run(y, parts, put(st1))

        def go_sum(self, *parts):
            go(SUM_IN, *parts)

        def go_y(self, *parts):
            go(Y_IN, *parts)

        def go_w(self, g):
            for h in range(2):
                w_inward(g, h).start()

        def out(self, *parts):
            self.plan.run(y, parts, put(rp))

        def final(self, *parts):
            final(SUM_OUT, parts, rp, r1)

    OUTER_UNIT = {"sum": "fo", "out": "no"}
    outer_plan = Plan([OUTER_UNIT[step[0]] for entry in SCHEDULE for step in entry[4] if step[0] in OUTER_UNIT])
    outer_work = Outer(outer_plan)

    begin(0)

    @pl.when(outer)
    def _():
        for h in range(2):
            w_inward(0, h).start()
        outer_plan.load(0)

    @pl.when(inner)
    def _():
        inner_plan.load(0)

    short_ref[...] = short_taps[...].astype(F32)
    for number, (k, start, stop, inner_steps, outer_steps) in enumerate(SCHEDULE):
        feature(k, start, stop)
        ending = number == len(SCHEDULE) - 1

        @pl.when(inner)
        def _():
            for step in inner_steps:
                if step[0] == "plane":
                    relay_plane(*step[1:])
                elif step[0] == "core":
                    relay_core(*step[1:])
                else:
                    getattr(inner_work, step[0])(*step[1:])
            if ending:
                settle()
                for part in range(len(PARTS)):
                    moving(ACROSS_OUTER, part).wait_send()
                    moving(ACROSS_INNER, part).wait_send()
                    moving(SUM_OUT, part).wait_send()
                for g in range(2):
                    for h in range(2):
                        for i in range(3):
                            w_plane(g, h, i).wait_send()
                        for i in range(4):
                            w_core(g, h, i).wait_send()

        @pl.when(outer)
        def _():
            for step in outer_steps:
                getattr(outer_work, step[0])(*step[1:])
            if ending:
                settle()
                for part in range(len(PARTS)):
                    moving(SUM_IN, part).wait_send()
                    moving(Y_IN, part).wait_send()
                for g in range(2):
                    for h in range(2):
                        w_inward(g, h).wait_send()

    pl.when(s < 7)(rim_copy.wait_send)


SCHEDULE = (
    (0, 0, 11, (("plane", 0, 0),), ()),
    (0, 11, 16, (), (("sum", 0, 1), ("go_sum", 0, 1))),
    (1, 0, 8, (("plane", 0, 1),), ()),
    (1, 8, 15, (("cross", 0),), ()),
    (1, 15, 16, (), (("sum", 2), ("go_sum", 2), ("go_y", 0, 1, 2))),
    (2, 0, 2, (("cross", 1),), ()),
    (2, 2, 11, (("core", 0, 0), ("cross", 2)), ()),
    (2, 11, 16, (("core", 0, 1), ("far", 0, 1, 2), ("far_end", 0, 1)), (("sum", 3, 4), ("go_sum", 3, 4))),
    (3, 0, 6, (("far_end", 2), ("cross", 3)), ()),
    (3, 6, 11, (("cross", 4), ("out", 0, 1, 2)), ()),
    (3, 11, 16, (), (("sum", 5, 6), ("go_sum", 5, 6))),
    (4, 0, 4, (("cross", 5),), ()),
    (4, 4, 12, (("cross", 6),), ()),
    (4, 12, 16, (
        ("far", 3, 4), ("near", 0, 1, 2), ("far_end", 3), ("out", 3, 4), ("near", 3, 4), ("far_end", 4), ("plane", 1, 0), ("far", 5, 6), ("near", 5, 6),
        ("plane", 1, 1), ("out", 5, 6), ("cross", 7), ("core", 1, 0), ("cross", 8), ("cross", 9), ("near", 7, 8, 9), ("far_end", 5), ("out", 7, 8, 9),
        ("far", 7, 8, 9), ("core", 1, 1), ("far_end", 6), ("near_end", 0, 1, 2), ("near_end", 3, 4), ("final", 0, 1, 2), ("far_end", 7), ("near_end", 5, 6), ("far_end", 8), ("final", 3, 4),
        ("far_end", 9), ("near_end", 7, 8, 9), ("final", 5, 6), ("final", 7), ("final", 8, 9),
    ), (
        ("sum", 7, 8, 9), ("go_y", 3, 4), ("go_w", 1), ("go_sum", 7, 8, 9), ("go_y", 5, 6, 7, 8, 9),
        ("out", 0, 1, 2), ("out", 3, 4), ("out", 5, 6), ("out", 7, 8, 9),
        ("final", 0, 1, 2), ("final", 3, 4), ("final", 5, 6), ("final", 7, 8, 9),
    )),
)


def lined(qkv, short_taps, medium_taps, skip_gain, w_out, resid, steer):
    channels, slab = qkv.shape[1:]
    width = resid.shape[0]
    whole = pl.BlockSpec(memory_space=pltpu.VMEM)
    anywhere = pl.BlockSpec(memory_space=pl.ANY)
    token = lambda: pltpu.VMEM((slab, channels), BF16)
    dma = pltpu.SemaphoreType.DMA
    span = 512
    return pl.pallas_call(
        line_kernel,
        in_specs=[anywhere] * 3 + [whole] * 4,
        out_specs=[anywhere] * 4,
        out_shape=[
            jax.ShapeDtypeStruct(resid.shape, BF16),
            jax.ShapeDtypeStruct((channels, width), BF16),
            jax.ShapeDtypeStruct((channels, width), BF16),
            jax.ShapeDtypeStruct((3, channels, 256), BF16),
        ],
        scratch_shapes=[token() for _ in range(8)]
        + [
            pltpu.VMEM((2, width // COLS, channels, COLS), BF16),
            pltpu.VMEM((2, 3, LANES, span), BF16),
            pltpu.VMEM((2, width, 256), BF16),
            pltpu.VMEM((3, STAPS, channels), F32),
            pltpu.VMEM((9 * PHASE, channels), F32),
            pltpu.VMEM((LANES, channels), F32),
            pltpu.VMEM((3, span, LANES), F32),
            pltpu.VMEM((span - LANES, LANES), F32),
            pltpu.VMEM((9, EDGE + (span - LANES) // 4, LANES), F32),
            pltpu.VMEM((EDGE + 64, LANES), F32),
            pltpu.VMEM((256, LANES), F32),
            dma((5, len(PARTS))),
            dma((5, len(PARTS))),
            dma((2, 2, 8)),
            dma((2, 2, 8)),
            dma,
            dma,
            dma((2, width // COLS)),
            dma((2, 2)),
            dma((2, 2)),
        ],
        compiler_params=pltpu.CompilerParams(
            collective_id=0, has_side_effects=True, vmem_limit_bytes=VMEM_LIMIT
        ),
        cost_estimate=pl.CostEstimate(
            flops=12 * channels * slab * width, bytes_accessed=20 * channels * width, transcendentals=0
        ),
    )(qkv, w_out, resid, jnp.swapaxes(short_taps, 1, 2), medium_taps, skip_gain[None], steer[None])[0]


def solution(mesh):
    line = mesh.shape["mp"] == 4 and mesh.shape["seq"] == 8
    return jax.shard_map(
        lined if line else shards,
        mesh=mesh,
        in_specs=(
            P(None, "mp", "seq"),
            P(None, "mp", None),
            P("mp", None),
            P("mp"),
            P("mp", None),
            P("mp", "seq"),
            P("mp"),
        ),
        out_specs=P("mp", "seq"),
        check_vma=False,
    )
```

```python
import functools

import jax
import jax.numpy as jnp
from jax import lax
from jax.experimental import pallas as pl
from jax.experimental.pallas import tpu as pltpu
from jax.sharding import PartitionSpec as P

STAPS = 7
MTAPS = 128
LANES = 128
F32 = jnp.float32
BF16 = jnp.bfloat16
MESH = pl.DeviceIdType.MESH


def from_behind(value, axis, steps):
    count = lax.axis_size(axis)
    return lax.ppermute(value, axis, [(source, source + steps) for source in range(count - steps)])


def chunks(slab):
    sizes = [1]
    left = slab // LANES - 3
    while left > 0:
        sizes.append(min(left, 2 if len(sizes) == 1 else 3))
        left -= sizes[-1]
    sizes.append(2)
    plan, end = [], slab
    for size in sizes:
        end -= size * LANES
        plan.append((end, size * LANES))
    return plan


def feature_kernel(blocks, *refs):
    token_refs = refs[:blocks]
    short_ref, medium_ref, y_ref, wide, kv = refs[blocks:]
    for at, ref in enumerate(token_refs):
        for s in range(3):
            if s > 0 or at > 0:
                wide[s, at * LANES : (at + 1) * LANES] = ref[s].astype(F32).T

    def short(s, row):
        total = short_ref[s, 0:1] * wide[s, row : row + LANES]
        for j in range(1, STAPS):
            total = total + short_ref[s, j : j + 1] * wide[s, row - j : row - j + LANES]
        return total

    for at in range(1, blocks):
        row = at * LANES
        kv[row - LANES : row] = (short(1, row) * short(2, row)).astype(BF16).astype(F32)

    for at in range(blocks - 2):
        row = at * LANES
        total = jnp.zeros((LANES, LANES), F32)
        for low in range(8):
            start = row + 8 - low
            block = kv[start : start + LANES + MTAPS - 8]
            for high in range(0, MTAPS, 8):
                first = MTAPS - 8 - high
                total = total + medium_ref[high + low : high + low + 1] * block[first : first + LANES]
        y_ref[row : row + LANES] = (short(0, row + 2 * LANES) * total).astype(BF16)


def features(sources, short, medium):
    channels = short.shape[2]
    blocks = len(sources)
    tokens = (blocks - 2) * LANES
    return pl.pallas_call(
        functools.partial(feature_kernel, blocks),
        grid=(channels // LANES,),
        in_specs=[pl.BlockSpec((3, LANES, LANES), lambda c, at=at: (0, c, at)) for _, at in sources]
        + [
            pl.BlockSpec((3, STAPS, LANES), lambda c: (0, 0, c)),
            pl.BlockSpec((MTAPS, LANES), lambda c: (0, c)),
        ],
        out_specs=pl.BlockSpec((tokens, LANES), lambda c: (0, c)),
        out_shape=jax.ShapeDtypeStruct((tokens, channels), BF16),
        scratch_shapes=[
            pltpu.VMEM((3, blocks * LANES, LANES), F32),
            pltpu.VMEM(((blocks - 1) * LANES, LANES), F32),
        ],
        cost_estimate=pl.CostEstimate(
            flops=2 * channels * tokens * (MTAPS + 4 * STAPS),
            bytes_accessed=6 * channels * blocks * LANES,
            transcendentals=0,
        ),
    )(*[array for array, _ in sources], short, medium)


def finish_kernel(*refs):
    resid_ref, steer_ref, proj_ref, out_ref = refs[0], refs[1], refs[2], refs[-1]
    gain = proj_ref[...].astype(F32) + steer_ref[...]
    out_ref[...] = (resid_ref[...].astype(F32) + gain.T).astype(BF16)


def finish(resid, steer, proj, out, first):
    tokens, channels = proj.shape
    rows = min(channels, 1024)
    at = first // LANES
    column = pl.BlockSpec((rows, LANES), lambda t, c: (c, at + t))
    specs = [
        column,
        pl.BlockSpec((1, rows), lambda t, c: (0, c)),
        pl.BlockSpec((LANES, rows), lambda t, c: (t, c)),
    ]
    held = [] if out is None else [out]
    return pl.pallas_call(
        finish_kernel,
        grid=(tokens // LANES, channels // rows),
        in_specs=specs + [pl.BlockSpec(memory_space=pl.ANY)] * len(held),
        out_specs=column,
        out_shape=jax.ShapeDtypeStruct(resid.shape, BF16),
        input_output_aliases={3: 0} if held else {},
        cost_estimate=pl.CostEstimate(
            flops=2 * channels * tokens, bytes_accessed=6 * channels * tokens, transcendentals=0
        ),
    )(resid, steer, proj, *held)


def shards(qkv, short_taps, medium_taps, skip_gain, w_out, resid, steer):
    slab = qkv.shape[2]
    short = jnp.swapaxes(short_taps.astype(F32), 1, 2)
    medium = medium_taps.astype(F32)
    medium = jnp.concatenate([medium[:, :1] + skip_gain[:, None], medium[:, 1:]], 1).T
    rim = from_behind(qkv[:, :, slab - 2 * LANES :], "seq", 1)
    out = None
    projs = []
    for first, tokens in chunks(slab):
        at = first // LANES
        sources = [(rim, i + 2) if i < 0 else (qkv, i) for i in range(at - 2, at + tokens // LANES)]
        y = features(sources, short, medium)
        part = jnp.dot(y, w_out, preferred_element_type=F32).astype(BF16)
        proj = lax.psum_scatter(part, "mp", scatter_dimension=1, tiled=True)
        projs.append((first, proj))
    for first, proj in projs:
        out = finish(resid, steer[None], proj, out, first)
    return out


PHASE = MTAPS // 4
EDGE = 8
COLS = 512
VMEM_LIMIT = 62 << 20
FEATURES = ((896, 128), (768, 128), (512, 256), (256, 256), (0, 256))
PARTS = (
    (960, 64), (896, 64), (832, 64), (768, 64), (640, 128), (512, 128), (384, 128), (256, 128),
    (192, 64), (128, 64), (64, 64), (0, 64),
)
PLANE = (2, 4, 6)
SUM_IN, Y_IN, ACROSS_OUTER, ACROSS_INNER, SUM_OUT = range(5)


def split_taps(c, lanes, medium_ref, skip_ref, nine, spare):
    spare[0:MTAPS] = medium_ref[pl.ds(pl.multiple_of(c * LANES, LANES), LANES)].astype(F32).T
    spare[0:1] = spare[0:1] + skip_ref[0:1, lanes]
    phase = [spare[pl.ds(p, PHASE, stride=4)] for p in range(4)]
    even = [phase[0], phase[2], phase[0] + phase[2]]
    odd = [phase[1], phase[3], phase[1] + phase[3]]
    for i, x in enumerate(even + odd + [a + b for a, b in zip(even, odd)]):
        nine[i * PHASE : (i + 1) * PHASE, lanes] = x


def filtered(blocks, known, kept, short_ref, nine_ref, top, lanes, wide, kv, xs, back, med):
    count = (blocks - 2) * LANES // 4
    held = (blocks - 1) * LANES // 4

    def short(s, row):
        total = short_ref[s, 0:1, lanes] * wide[s, row : row + LANES]
        for j in range(1, STAPS):
            total = total + short_ref[s, j : j + 1, lanes] * wide[s, row - j : row - j + LANES]
        return total

    for at in range(1, blocks - 1 if known else blocks):
        row = at * LANES
        kv[row - LANES : row] = (short(1, row) * short(2, row)).astype(BF16).astype(F32)
    if known:
        kv[(blocks - 2) * LANES : (blocks - 1) * LANES] = top[:, lanes]
    if kept:
        top[:, lanes] = kv[0:LANES]
    phase = [kv[pl.ds(p, held, stride=4)] for p in range(4)]
    even = [phase[0], phase[2], phase[0] + phase[2]]
    odd = [phase[1], phase[3], phase[1] + phase[3]]
    for i, x in enumerate(even + odd + [a + b for a, b in zip(even, odd)]):
        xs[i, EDGE : EDGE + held] = x

    def conv(i, edge):
        size, total = count + edge, None
        for low in range(8):
            start = EDGE + 8 - edge - low
            block = xs[i, start : start + size + PHASE - 8]
            for high in range(0, PHASE, 8):
                first = PHASE - 8 - high
                tap = i * PHASE + high + low
                term = nine_ref[tap : tap + 1, lanes] * block[first : first + size]
                total = term if total is None else total + term
        return total

    def delayed(value):
        back[0 : count + EDGE] = value
        return back[EDGE - 1 : EDGE - 1 + count]

    def pair(g, edge):
        first, second, both = conv(3 * g, edge), conv(3 * g + 1, EDGE), conv(3 * g + 2, edge)
        return first[edge:] + delayed(second), both - first - second[EDGE - edge :]

    odd0, odd1 = pair(1, EDGE)
    late, odd1 = delayed(odd1), odd1[EDGE:]
    even0, even1 = pair(0, 0)
    both0, both1 = pair(2, 0)
    med[pl.ds(0, count, stride=4)] = even0 + late
    med[pl.ds(1, count, stride=4)] = both0 - even0 - odd0
    med[pl.ds(2, count, stride=4)] = even1 + odd0
    med[pl.ds(3, count, stride=4)] = both1 - even1 - odd1
    for at in range(blocks - 2):
        row = at * LANES
        yield row, (short(0, row + 2 * LANES) * med[row : row + LANES]).astype(BF16)


def line_kernel(
    qkv, w_out, resid, short_taps, medium_ref, skip_ref, steer_ref,
    out, wx_far, wx_near, rim,
    y, yx, st1, st2, st3, r1, rp, rq, wbuf, qbuf, rbuf, short_ref, nine_ref, top, wide, kv, xs, back, med,
    send, recv, w_send, w_recv, rim_send, rim_recv, fetch_sem, q_sem, r_sem,
):
    s, m = lax.axis_index("seq"), lax.axis_index("mp")
    channels, slab = qkv.shape[1], qkv.shape[2]
    width = resid.shape[0]
    steps = width // COLS
    low = m < 2
    inner = jnp.logical_or(m == 1, m == 2)
    outer = jnp.logical_not(inner)
    far_outer, far_inner = jnp.where(low, 3, 0), jnp.where(low, 2, 1)
    near_inner, near_outer = jnp.where(low, 1, 2), jnp.where(low, 0, 3)
    inward = (s, near_inner)
    outward = (s, near_outer)
    opposite = (s, jnp.where(low, 2, 1))

    barrier = pltpu.get_barrier_semaphore()

    def greet(condition, device):
        @pl.when(condition)
        def _():
            pl.semaphore_signal(barrier, inc=1, device_id=device, device_id_type=MESH)

    greet(m < 3, (s, jnp.minimum(m + 1, 3)))
    greet(m > 0, (s, jnp.maximum(m - 1, 0)))
    greet(s < 7, (jnp.minimum(s + 1, 7), m))
    greet(s > 0, (jnp.maximum(s - 1, 0), m))
    for flip in (1, *PLANE):
        pl.semaphore_signal(barrier, inc=1, device_id=(s ^ flip, m), device_id_type=MESH)
    one = lambda c: jnp.where(c, 1, 0)
    pl.semaphore_wait(barrier, 4 + one(m < 3) + one(m > 0) + one(s < 7) + one(s > 0))

    def remote(src, dst, sent, got, device):
        return pltpu.make_async_remote_copy(
            src_ref=src, dst_ref=dst, send_sem=sent, recv_sem=got, device_id=device, device_id_type=MESH
        )

    rim_copy = remote(qkv.at[:, :, slab - 256 : slab], rim, rim_send, rim_recv, (jnp.minimum(s + 1, 7), m))
    pl.when(s < 7)(rim_copy.start)

    share = channels // 16
    held = (wx_far, wx_near)

    def rows_of(device, h):
        return pl.ds(pl.multiple_of((device * 2 + h) * share, share), share)

    def w_inward(g, h):
        group = (far_inner, near_inner)[g]
        columns = pl.ds(pl.multiple_of(group * width, width), width)
        return remote(
            w_out.at[rows_of(s, h), columns], held[g].at[rows_of(s, h)], w_send.at[g, h, 0], w_recv.at[g, h, 0], inward
        )

    def w_plane(g, h, i):
        mine = held[g].at[rows_of(s, h)]
        return remote(mine, mine, w_send.at[g, h, 1 + i], w_recv.at[g, h, 1 + i], (s ^ PLANE[i], m))

    def w_core(g, h, i):
        piece = held[g].at[rows_of(s if i == 0 else s ^ PLANE[i - 1], h)]
        return remote(piece, piece, w_send.at[g, h, 4 + i], w_recv.at[g, h, 4 + i], (s ^ 1, m))

    def relay_plane(g, h):
        w_inward(g, h).wait_recv()
        for i in range(3):
            w_plane(g, h, i).start()
        w_core(g, h, 0).start()

    def relay_core(g, h):
        for i in range(3):
            w_plane(g, h, i).wait_recv()
            w_core(g, h, 1 + i).start()

    def relay_end(g):
        for h in range(2):
            for i in range(4):
                w_core(g, h, i).wait_recv()

    def rows(k):
        return pl.ds(PARTS[k][0], PARTS[k][1])

    def moving(kind, k):
        src, dst, device = {
            SUM_IN: (st1, r1, inward),
            Y_IN: (y, yx, inward),
            ACROSS_OUTER: (st1, rp, opposite),
            ACROSS_INNER: (st2, rq, opposite),
            SUM_OUT: (st3, r1, outward),
        }[kind]
        return remote(src.at[rows(k)], dst.at[rows(k)], send.at[kind, k], recv.at[kind, k], device)

    def fetch(which, half, j):
        if which in (0, 1):
            block = held[which].at[:, pl.ds(pl.multiple_of(j * COLS, COLS), COLS)]
        else:
            group = {"fo": far_outer, "fi": far_inner, "ni": near_inner, "no": near_outer}[which]
            block = w_out.at[:, pl.ds(pl.multiple_of(group * width + j * COLS, COLS), COLS)]
        return pltpu.make_async_copy(block, wbuf.at[half, j], fetch_sem.at[half, j])

    class Plan:
        def __init__(self, units):
            self.units, self.at, self.ended = units, 0, set()

        def load(self, i):
            if i < len(self.units):
                which = self.units[i]
                if which in (0, 1) and which not in self.ended:
                    self.ended.add(which)
                    relay_end(which)
                for j in range(steps):
                    fetch(which, i % 2, j).start()

        def run(self, src, parts, each):
            i = self.at
            self.at += 1
            self.load(i + 1)
            first = PARTS[parts[-1]][0]
            tokens = sum(PARTS[k][1] for k in parts)

            def body(j, carry):
                fetch(self.units[i], i % 2, j).wait()
                total = jnp.dot(src[first : first + tokens], wbuf[i % 2, j], preferred_element_type=F32)
                each(total, j, pl.ds(first, tokens), pl.ds(pl.multiple_of(j * COLS, COLS), COLS))
                return carry

            lax.fori_loop(0, steps, body, 0)

    def put(dst, *adds):
        def each(total, j, at, columns):
            for ref in adds:
                total = total + ref[at, columns].astype(F32)
            dst[at, columns] = total.astype(BF16)

        return each

    def resid_in(slot, first, tokens):
        return pltpu.make_async_copy(
            resid.at[:, first : first + tokens], rbuf.at[slot, :, 0:tokens], r_sem.at[0, slot]
        )

    def out_of(slot, first, tokens):
        return pltpu.make_async_copy(
            rbuf.at[slot, :, 0:tokens], out.at[:, first : first + tokens], r_sem.at[1, slot]
        )

    leaving = []

    def final(kind, parts, left, right):
        first = PARTS[parts[-1]][0]
        tokens = sum(PARTS[k][1] for k in parts)
        slot = len(leaving) % 2
        if len(leaving) >= 2:
            out_of(*leaving[-2]).wait()
        resid_in(slot, first, tokens).start()
        leaving.append((slot, first, tokens))
        wait_in(kind, *parts)
        resid_in(slot, first, tokens).wait()
        at = pl.ds(first, tokens)

        def body(j, carry):
            columns = pl.ds(pl.multiple_of(j * COLS, COLS), COLS)
            total = left[at, columns].astype(F32) + right[at, columns].astype(F32) + steer_ref[0:1, columns]
            rbuf[slot, columns, 0:tokens] = (rbuf[slot, columns, 0:tokens].astype(F32) + total.T).astype(BF16)
            return carry

        lax.fori_loop(0, steps, body, 0)
        out_of(slot, first, tokens).start()

    def settle():
        for left in leaving[-2:]:
            out_of(*left).wait()
        leaving.clear()

    blocks_of_channels = channels // LANES

    def load(k, c, slot, act):
        first, tokens = FEATURES[k]
        span = tokens + 256
        lanes = pl.ds(pl.multiple_of(c * LANES, LANES), LANES)
        if first > 0:
            act(pltpu.make_async_copy(
                qkv.at[:, lanes, first - 256 : first + tokens], qbuf.at[slot, :, :, 0:span], q_sem.at[0, slot]
            ))
        else:
            act(pltpu.make_async_copy(
                qkv.at[:, lanes, 0:tokens], qbuf.at[slot, :, :, 256:span], q_sem.at[0, slot]
            ))

            @pl.when(s > 0)
            def _():
                act(pltpu.make_async_copy(rim.at[:, lanes], qbuf.at[slot, :, :, 0:256], q_sem.at[1, slot]))

    def begin(k):
        if FEATURES[k][0] == 0:

            @pl.when(s > 0)
            def _():
                rim_copy.wait_recv()

            @pl.when(s == 0)
            def _():
                qbuf[:, :, :, 0:256] = jnp.zeros((2, 3, LANES, 256), BF16)

        load(k, 0, 0, lambda copy: copy.start())

    def feature(k, start, stop):
        first, tokens = FEATURES[k]
        blocks = (tokens + 256) // LANES
        known, kept = k > 0, k + 1 < len(FEATURES)

        def body(c, carry):
            slot = lax.rem(c, 2)

            @pl.when(c + 1 < blocks_of_channels)
            def _():
                load(k, c + 1, 1 - slot, lambda copy: copy.start())

            load(k, c, slot, lambda copy: copy.wait())
            lanes = pl.ds(pl.multiple_of(c * LANES, LANES), LANES)
            if k == 0:
                split_taps(c, lanes, medium_ref, skip_ref, nine_ref, med)
            for at in range(blocks):
                for i in range(3):
                    if at > 0 if i == 0 else not (known and at == blocks - 1):
                        wide[i, at * LANES : (at + 1) * LANES] = (
                            qbuf[slot, i, :, at * LANES : (at + 1) * LANES].astype(F32).T
                        )
            pieces = filtered(
                blocks, known, kept, short_ref, nine_ref, top, lanes, wide, kv, xs, back, med
            )
            for row, value in pieces:
                y[first + row : first + row + LANES, lanes] = value
            return carry

        lax.fori_loop(start, stop, body, 0)
        if stop == blocks_of_channels and k + 1 < len(FEATURES):
            begin(k + 1)

    def wait_in(kind, *parts):
        for k in parts:
            moving(kind, k).wait_recv()

    def go(kind, *parts):
        for k in parts:
            moving(kind, k).start()

    class Inner:
        def __init__(self, plan):
            self.plan = plan

        def cross(self, *parts):
            wait_in(SUM_IN, *parts)
            self.plan.run(y, parts, put(st1, r1))
            go(ACROSS_OUTER, *parts)

        def far(self, *parts):
            self.plan.run(y, parts, put(st2))

        def far_end(self, *parts):
            wait_in(Y_IN, *parts)
            self.plan.run(yx, parts, put(st2, st2))
            go(ACROSS_INNER, *parts)

        def out(self, *parts):
            wait_in(ACROSS_OUTER, *parts)
            self.plan.run(y, parts, put(st3, rp))
            go(SUM_OUT, *parts)

        def near(self, *parts):
            self.plan.run(y, parts, put(r1))

        def near_end(self, *parts):
            self.plan.run(yx, parts, put(r1, r1))

        def final(self, *parts):
            final(ACROSS_INNER, parts, r1, rq)

    UNIT = {"cross": "fo", "far": "fi", "far_end": 0, "out": "no", "near": "ni", "near_end": 1}
    inner_plan = Plan([UNIT[step[0]] for entry in SCHEDULE for step in entry[3] if step[0] in UNIT])
    inner_work = Inner(inner_plan)

    class Outer:
        def __init__(self, plan):
            self.plan = plan

        def sum(self, *parts):
            self.plan.run(y, parts, put(st1))

        def go_sum(self, *parts):
            go(SUM_IN, *parts)

        def go_y(self, *parts):
            go(Y_IN, *parts)

        def out(self, *parts):
            self.plan.run(y, parts, put(rp))

        def final(self, *parts):
            final(SUM_OUT, parts, rp, r1)

    OUTER_UNIT = {"sum": "fo", "out": "no"}
    outer_plan = Plan([OUTER_UNIT[step[0]] for entry in SCHEDULE for step in entry[4] if step[0] in OUTER_UNIT])
    outer_work = Outer(outer_plan)

    begin(0)

    @pl.when(outer)
    def _():
        for g in range(2):
            for h in range(2):
                w_inward(g, h).start()
        outer_plan.load(0)

    @pl.when(inner)
    def _():
        inner_plan.load(0)

    short_ref[...] = short_taps[...].astype(F32)
    for number, (k, start, stop, inner_steps, outer_steps) in enumerate(SCHEDULE):
        feature(k, start, stop)
        ending = number == len(SCHEDULE) - 1

        @pl.when(inner)
        def _():
            for step in inner_steps:
                if step[0] == "plane":
                    relay_plane(*step[1:])
                elif step[0] == "core":
                    relay_core(*step[1:])
                else:
                    getattr(inner_work, step[0])(*step[1:])
            if ending:
                settle()
                for part in range(len(PARTS)):
                    moving(ACROSS_OUTER, part).wait_send()
                    moving(ACROSS_INNER, part).wait_send()
                    moving(SUM_OUT, part).wait_send()
                for g in range(2):
                    for h in range(2):
                        for i in range(3):
                            w_plane(g, h, i).wait_send()
                        for i in range(4):
                            w_core(g, h, i).wait_send()

        @pl.when(outer)
        def _():
            for step in outer_steps:
                getattr(outer_work, step[0])(*step[1:])
            if ending:
                settle()
                for part in range(len(PARTS)):
                    moving(SUM_IN, part).wait_send()
                    moving(Y_IN, part).wait_send()
                for g in range(2):
                    for h in range(2):
                        w_inward(g, h).wait_send()

    pl.when(s < 7)(rim_copy.wait_send)


SCHEDULE = (
    (0, 0, 11, (("plane", 0, 0),), ()),
    (0, 11, 16, (), (("sum", 0, 1), ("go_sum", 0, 1))),
    (1, 0, 8, (("plane", 0, 1),), ()),
    (1, 8, 16, (), (("sum", 2, 3), ("go_sum", 2, 3), ("go_y", 0, 1, 2, 3))),
    (2, 0, 5, (("plane", 1, 0), ("core", 0, 0)), ()),
    (2, 5, 12, (("plane", 1, 1), ("far", 0, 1, 2, 3)), ()),
    (2, 12, 14, (("cross", 0),), ()),
    (2, 14, 16, (("cross", 1), ("core", 0, 1)), (("sum", 4, 5), ("go_sum", 4, 5), ("go_y", 4, 5))),
    (3, 0, 2, (("cross", 2),), ()),
    (3, 2, 5, (("cross", 3),), ()),
    (3, 5, 8, (("far_end", 0), ("far_end", 1)), ()),
    (3, 8, 11, (("far_end", 2),), ()),
    (3, 11, 15, (("far_end", 3), ("out", 0, 1, 2, 3)), ()),
    (3, 15, 16, (("cross", 4),), (("sum", 6, 7), ("go_sum", 6, 7))),
    (4, 0, 3, (("core", 1, 0),), ()),
    (4, 3, 8, (("core", 1, 1), ("cross", 5), ("far", 4, 5)), ()),
    (4, 8, 12, (("far_end", 4),), ()),
    (4, 12, 16, (
        ("near", 0, 1, 2, 3), ("far_end", 5), ("near_end", 0, 1, 2, 3), ("out", 4, 5), ("cross", 6), ("final", 0, 1, 2, 3),
        ("near", 4, 5), ("cross", 7), ("near_end", 4, 5), ("cross", 8), ("cross", 9), ("final", 4, 5), ("cross", 10), ("out", 6, 7), ("cross", 11), ("far", 6, 7), ("near", 6, 7),
        ("far_end", 6), ("near", 8, 9, 10, 11), ("out", 8, 9, 10, 11), ("far_end", 7), ("near_end", 6, 7),
        ("far", 8, 9, 10, 11), ("far_end", 8), ("far_end", 9), ("final", 6, 7), ("far_end", 10), ("far_end", 11), ("near_end", 8, 9, 10, 11), ("final", 8, 9), ("final", 10, 11),
    ), (
        ("sum", 8, 9, 10, 11), ("go_sum", 8, 9, 10, 11), ("go_y", 6, 7, 8, 9, 10, 11),
        ("out", 0, 1, 2, 3), ("out", 4, 5), ("out", 6, 7), ("out", 8, 9, 10, 11),
        ("final", 0, 1, 2, 3), ("final", 4, 5), ("final", 6, 7), ("final", 8, 9, 10, 11),
    )),
)


def copy_kernel(source_ref, out_ref):
    out_ref[...] = source_ref[...]


def copied(value):
    rows, columns = value.shape
    block = pl.BlockSpec((rows // 8, columns), lambda i: (i, 0))
    return pl.pallas_call(
        copy_kernel,
        grid=(8,),
        in_specs=[block],
        out_specs=block,
        out_shape=jax.ShapeDtypeStruct(value.shape, value.dtype),
        cost_estimate=pl.CostEstimate(flops=0, bytes_accessed=4 * rows * columns, transcendentals=0),
    )(value)


def lined(qkv, short_taps, medium_taps, skip_gain, w_out, resid, steer):
    channels, slab = qkv.shape[1:]
    width = resid.shape[0]
    whole = pl.BlockSpec(memory_space=pltpu.VMEM)
    anywhere = pl.BlockSpec(memory_space=pl.ANY)
    token = lambda: pltpu.VMEM((slab, channels), BF16)
    dma = pltpu.SemaphoreType.DMA
    span = 512
    result = pl.pallas_call(
        line_kernel,
        in_specs=[anywhere] * 3 + [whole] * 4,
        out_specs=[anywhere] * 4,
        out_shape=[
            jax.ShapeDtypeStruct(resid.shape, BF16),
            jax.ShapeDtypeStruct((channels, width), BF16),
            jax.ShapeDtypeStruct((channels, width), BF16),
            jax.ShapeDtypeStruct((3, channels, 256), BF16),
        ],
        scratch_shapes=[token() for _ in range(8)]
        + [
            pltpu.VMEM((2, width // COLS, channels, COLS), BF16),
            pltpu.VMEM((2, 3, LANES, span), BF16),
            pltpu.VMEM((2, width, 256), BF16),
            pltpu.VMEM((3, STAPS, channels), F32),
            pltpu.VMEM((9 * PHASE, channels), F32),
            pltpu.VMEM((LANES, channels), F32),
            pltpu.VMEM((3, span, LANES), F32),
            pltpu.VMEM((span - LANES, LANES), F32),
            pltpu.VMEM((9, EDGE + (span - LANES) // 4, LANES), F32),
            pltpu.VMEM((EDGE + 64, LANES), F32),
            pltpu.VMEM((256, LANES), F32),
            dma((5, len(PARTS))),
            dma((5, len(PARTS))),
            dma((2, 2, 8)),
            dma((2, 2, 8)),
            dma,
            dma,
            dma((2, width // COLS)),
            dma((2, 2)),
            dma((2, 2)),
        ],
        compiler_params=pltpu.CompilerParams(
            collective_id=0, has_side_effects=True, vmem_limit_bytes=VMEM_LIMIT
        ),
        cost_estimate=pl.CostEstimate(
            flops=12 * channels * slab * width, bytes_accessed=20 * channels * width, transcendentals=0
        ),
    )(qkv, w_out, resid, jnp.swapaxes(short_taps, 1, 2), medium_taps, skip_gain[None], steer[None])[0]
    return copied(result)


def solution(mesh):
    line = mesh.shape["mp"] == 4 and mesh.shape["seq"] == 8
    return jax.shard_map(
        lined if line else shards,
        mesh=mesh,
        in_specs=(
            P(None, "mp", "seq"),
            P(None, "mp", None),
            P("mp", None),
            P("mp"),
            P("mp", None),
            P("mp", "seq"),
            P("mp"),
        ),
        out_specs=P("mp", "seq"),
        check_vma=False,
    )
```

```python
import functools

import jax
import jax.numpy as jnp
from jax import lax
from jax.experimental import pallas as pl
from jax.experimental.pallas import tpu as pltpu
from jax.sharding import PartitionSpec as P

STAPS = 7
MTAPS = 128
LANES = 128
F32 = jnp.float32
BF16 = jnp.bfloat16
MESH = pl.DeviceIdType.MESH


def from_behind(value, axis, steps):
    count = lax.axis_size(axis)
    return lax.ppermute(value, axis, [(source, source + steps) for source in range(count - steps)])


def chunks(slab):
    sizes = [1]
    left = slab // LANES - 3
    while left > 0:
        sizes.append(min(left, 2 if len(sizes) == 1 else 3))
        left -= sizes[-1]
    sizes.append(2)
    plan, end = [], slab
    for size in sizes:
        end -= size * LANES
        plan.append((end, size * LANES))
    return plan


def feature_kernel(blocks, *refs):
    token_refs = refs[:blocks]
    short_ref, medium_ref, y_ref, wide, kv = refs[blocks:]
    for at, ref in enumerate(token_refs):
        for s in range(3):
            if s > 0 or at > 0:
                wide[s, at * LANES : (at + 1) * LANES] = ref[s].astype(F32).T

    def short(s, row):
        total = short_ref[s, 0:1] * wide[s, row : row + LANES]
        for j in range(1, STAPS):
            total = total + short_ref[s, j : j + 1] * wide[s, row - j : row - j + LANES]
        return total

    for at in range(1, blocks):
        row = at * LANES
        kv[row - LANES : row] = (short(1, row) * short(2, row)).astype(BF16).astype(F32)

    for at in range(blocks - 2):
        row = at * LANES
        total = jnp.zeros((LANES, LANES), F32)
        for low in range(8):
            start = row + 8 - low
            block = kv[start : start + LANES + MTAPS - 8]
            for high in range(0, MTAPS, 8):
                first = MTAPS - 8 - high
                total = total + medium_ref[high + low : high + low + 1] * block[first : first + LANES]
        y_ref[row : row + LANES] = (short(0, row + 2 * LANES) * total).astype(BF16)


def features(sources, short, medium):
    channels = short.shape[2]
    blocks = len(sources)
    tokens = (blocks - 2) * LANES
    return pl.pallas_call(
        functools.partial(feature_kernel, blocks),
        grid=(channels // LANES,),
        in_specs=[pl.BlockSpec((3, LANES, LANES), lambda c, at=at: (0, c, at)) for _, at in sources]
        + [
            pl.BlockSpec((3, STAPS, LANES), lambda c: (0, 0, c)),
            pl.BlockSpec((MTAPS, LANES), lambda c: (0, c)),
        ],
        out_specs=pl.BlockSpec((tokens, LANES), lambda c: (0, c)),
        out_shape=jax.ShapeDtypeStruct((tokens, channels), BF16),
        scratch_shapes=[
            pltpu.VMEM((3, blocks * LANES, LANES), F32),
            pltpu.VMEM(((blocks - 1) * LANES, LANES), F32),
        ],
        cost_estimate=pl.CostEstimate(
            flops=2 * channels * tokens * (MTAPS + 4 * STAPS),
            bytes_accessed=6 * channels * blocks * LANES,
            transcendentals=0,
        ),
    )(*[array for array, _ in sources], short, medium)


def finish_kernel(*refs):
    resid_ref, steer_ref, proj_ref, out_ref = refs[0], refs[1], refs[2], refs[-1]
    gain = proj_ref[...].astype(F32) + steer_ref[...]
    out_ref[...] = (resid_ref[...].astype(F32) + gain.T).astype(BF16)


def finish(resid, steer, proj, out, first):
    tokens, channels = proj.shape
    rows = min(channels, 1024)
    at = first // LANES
    column = pl.BlockSpec((rows, LANES), lambda t, c: (c, at + t))
    specs = [
        column,
        pl.BlockSpec((1, rows), lambda t, c: (0, c)),
        pl.BlockSpec((LANES, rows), lambda t, c: (t, c)),
    ]
    held = [] if out is None else [out]
    return pl.pallas_call(
        finish_kernel,
        grid=(tokens // LANES, channels // rows),
        in_specs=specs + [pl.BlockSpec(memory_space=pl.ANY)] * len(held),
        out_specs=column,
        out_shape=jax.ShapeDtypeStruct(resid.shape, BF16),
        input_output_aliases={3: 0} if held else {},
        cost_estimate=pl.CostEstimate(
            flops=2 * channels * tokens, bytes_accessed=6 * channels * tokens, transcendentals=0
        ),
    )(resid, steer, proj, *held)


def shards(qkv, short_taps, medium_taps, skip_gain, w_out, resid, steer):
    slab = qkv.shape[2]
    short = jnp.swapaxes(short_taps.astype(F32), 1, 2)
    medium = medium_taps.astype(F32)
    medium = jnp.concatenate([medium[:, :1] + skip_gain[:, None], medium[:, 1:]], 1).T
    rim = from_behind(qkv[:, :, slab - 2 * LANES :], "seq", 1)
    out = None
    projs = []
    for first, tokens in chunks(slab):
        at = first // LANES
        sources = [(rim, i + 2) if i < 0 else (qkv, i) for i in range(at - 2, at + tokens // LANES)]
        y = features(sources, short, medium)
        part = jnp.dot(y, w_out, preferred_element_type=F32).astype(BF16)
        proj = lax.psum_scatter(part, "mp", scatter_dimension=1, tiled=True)
        projs.append((first, proj))
    for first, proj in projs:
        out = finish(resid, steer[None], proj, out, first)
    return out


PHASE = MTAPS // 4
EDGE = 8
COLS = 512
VMEM_LIMIT = 62 << 20
FEATURES = ((896, 128), (768, 128), (512, 256), (256, 256), (0, 256))
PARTS = (
    (960, 64), (896, 64), (768, 128), (640, 128), (512, 128), (384, 128), (256, 128), (128, 128), (64, 64), (0, 64),
)
PLANE = (2, 4, 6)
SUM_IN, Y_IN, ACROSS_OUTER, ACROSS_INNER, SUM_OUT = range(5)


def split_taps(c, lanes, medium_ref, skip_ref, nine, spare):
    spare[0:MTAPS] = medium_ref[pl.ds(pl.multiple_of(c * LANES, LANES), LANES)].astype(F32).T
    spare[0:1] = spare[0:1] + skip_ref[0:1, lanes]
    phase = [spare[pl.ds(p, PHASE, stride=4)] for p in range(4)]
    even = [phase[0], phase[2], phase[0] + phase[2]]
    odd = [phase[1], phase[3], phase[1] + phase[3]]
    for i, x in enumerate(even + odd + [a + b for a, b in zip(even, odd)]):
        nine[i * PHASE : (i + 1) * PHASE, lanes] = x


def filtered(blocks, known, kept, short_ref, nine_ref, top, lanes, wide, kv, xs, back, med):
    count = (blocks - 2) * LANES // 4
    held = (blocks - 1) * LANES // 4

    def short(s, row):
        total = short_ref[s, 0:1, lanes] * wide[s, row : row + LANES]
        for j in range(1, STAPS):
            total = total + short_ref[s, j : j + 1, lanes] * wide[s, row - j : row - j + LANES]
        return total

    for at in range(1, blocks - 1 if known else blocks):
        row = at * LANES
        kv[row - LANES : row] = (short(1, row) * short(2, row)).astype(BF16).astype(F32)
    if known:
        kv[(blocks - 2) * LANES : (blocks - 1) * LANES] = top[:, lanes]
    if kept:
        top[:, lanes] = kv[0:LANES]
    phase = [kv[pl.ds(p, held, stride=4)] for p in range(4)]
    even = [phase[0], phase[2], phase[0] + phase[2]]
    odd = [phase[1], phase[3], phase[1] + phase[3]]
    for i, x in enumerate(even + odd + [a + b for a, b in zip(even, odd)]):
        xs[i, EDGE : EDGE + held] = x

    def conv(i, edge):
        size, total = count + edge, None
        for low in range(8):
            start = EDGE + 8 - edge - low
            block = xs[i, start : start + size + PHASE - 8]
            for high in range(0, PHASE, 8):
                first = PHASE - 8 - high
                tap = i * PHASE + high + low
                term = nine_ref[tap : tap + 1, lanes] * block[first : first + size]
                total = term if total is None else total + term
        return total

    def delayed(value):
        back[0 : count + EDGE] = value
        return back[EDGE - 1 : EDGE - 1 + count]

    def pair(g, edge):
        first, second, both = conv(3 * g, edge), conv(3 * g + 1, EDGE), conv(3 * g + 2, edge)
        return first[edge:] + delayed(second), both - first - second[EDGE - edge :]

    odd0, odd1 = pair(1, EDGE)
    late, odd1 = delayed(odd1), odd1[EDGE:]
    even0, even1 = pair(0, 0)
    both0, both1 = pair(2, 0)
    med[pl.ds(0, count, stride=4)] = even0 + late
    med[pl.ds(1, count, stride=4)] = both0 - even0 - odd0
    med[pl.ds(2, count, stride=4)] = even1 + odd0
    med[pl.ds(3, count, stride=4)] = both1 - even1 - odd1
    for at in range(blocks - 2):
        row = at * LANES
        yield row, (short(0, row + 2 * LANES) * med[row : row + LANES]).astype(BF16)


def line_kernel(
    qkv, w_out, resid, short_taps, medium_ref, skip_ref, steer_ref,
    out, wx_far, wx_near, rim,
    y, yx, st1, st2, st3, r1, rp, rq, wbuf, qbuf, rbuf, short_ref, nine_ref, top, wide, kv, xs, back, med,
    send, recv, w_send, w_recv, rim_send, rim_recv, fetch_sem, q_sem, r_sem,
):
    s, m = lax.axis_index("seq"), lax.axis_index("mp")
    channels, slab = qkv.shape[1], qkv.shape[2]
    width = resid.shape[0]
    steps = width // COLS
    low = m < 2
    inner = jnp.logical_or(m == 1, m == 2)
    outer = jnp.logical_not(inner)
    far_outer, far_inner = jnp.where(low, 3, 0), jnp.where(low, 2, 1)
    near_inner, near_outer = jnp.where(low, 1, 2), jnp.where(low, 0, 3)
    inward = (s, near_inner)
    outward = (s, near_outer)
    opposite = (s, jnp.where(low, 2, 1))

    barrier = pltpu.get_barrier_semaphore()

    def greet(condition, device):
        @pl.when(condition)
        def _():
            pl.semaphore_signal(barrier, inc=1, device_id=device, device_id_type=MESH)

    greet(m < 3, (s, jnp.minimum(m + 1, 3)))
    greet(m > 0, (s, jnp.maximum(m - 1, 0)))
    greet(s < 7, (jnp.minimum(s + 1, 7), m))
    greet(s > 0, (jnp.maximum(s - 1, 0), m))
    for flip in (1, *PLANE):
        pl.semaphore_signal(barrier, inc=1, device_id=(s ^ flip, m), device_id_type=MESH)
    one = lambda c: jnp.where(c, 1, 0)
    pl.semaphore_wait(barrier, 4 + one(m < 3) + one(m > 0) + one(s < 7) + one(s > 0))

    def remote(src, dst, sent, got, device):
        return pltpu.make_async_remote_copy(
            src_ref=src, dst_ref=dst, send_sem=sent, recv_sem=got, device_id=device, device_id_type=MESH
        )

    rim_copy = remote(qkv.at[:, :, slab - 256 : slab], rim, rim_send, rim_recv, (jnp.minimum(s + 1, 7), m))
    pl.when(s < 7)(rim_copy.start)

    share = channels // 16
    held = (wx_far, wx_near)

    def rows_of(device, h):
        return pl.ds(pl.multiple_of((device * 2 + h) * share, share), share)

    def w_inward(g, h):
        group = (far_inner, near_inner)[g]
        columns = pl.ds(pl.multiple_of(group * width, width), width)
        return remote(
            w_out.at[rows_of(s, h), columns], held[g].at[rows_of(s, h)], w_send.at[g, h, 0], w_recv.at[g, h, 0], inward
        )

    def w_plane(g, h, i):
        mine = held[g].at[rows_of(s, h)]
        return remote(mine, mine, w_send.at[g, h, 1 + i], w_recv.at[g, h, 1 + i], (s ^ PLANE[i], m))

    def w_core(g, h, i):
        piece = held[g].at[rows_of(s if i == 0 else s ^ PLANE[i - 1], h)]
        return remote(piece, piece, w_send.at[g, h, 4 + i], w_recv.at[g, h, 4 + i], (s ^ 1, m))

    def relay_plane(g, h):
        w_inward(g, h).wait_recv()
        for i in range(3):
            w_plane(g, h, i).start()
        w_core(g, h, 0).start()

    def relay_core(g, h):
        for i in range(3):
            w_plane(g, h, i).wait_recv()
            w_core(g, h, 1 + i).start()

    def relay_end(g):
        for h in range(2):
            for i in range(4):
                w_core(g, h, i).wait_recv()

    def rows(k):
        return pl.ds(PARTS[k][0], PARTS[k][1])

    def moving(kind, k):
        src, dst, device = {
            SUM_IN: (st1, r1, inward),
            Y_IN: (y, yx, inward),
            ACROSS_OUTER: (st1, rp, opposite),
            ACROSS_INNER: (st2, rq, opposite),
            SUM_OUT: (st3, r1, outward),
        }[kind]
        return remote(src.at[rows(k)], dst.at[rows(k)], send.at[kind, k], recv.at[kind, k], device)

    def fetch(which, half, j):
        if which in (0, 1):
            block = held[which].at[:, pl.ds(pl.multiple_of(j * COLS, COLS), COLS)]
        else:
            group = {"fo": far_outer, "fi": far_inner, "ni": near_inner, "no": near_outer}[which]
            block = w_out.at[:, pl.ds(pl.multiple_of(group * width + j * COLS, COLS), COLS)]
        return pltpu.make_async_copy(block, wbuf.at[half, j], fetch_sem.at[half, j])

    class Plan:
        def __init__(self, units):
            self.units, self.at, self.ended = units, 0, set()
            self.turn, self.runs = [], []
            for which in units:
                if not self.runs or self.runs[-1] != which:
                    self.runs.append(which)
                self.turn.append(len(self.runs) - 1)

        def load(self, i):
            if i < len(self.runs):
                which = self.runs[i]
                if which in (0, 1) and which not in self.ended:
                    self.ended.add(which)
                    relay_end(which)
                for j in range(steps):
                    fetch(which, i % 2, j).start()

        def run(self, src, parts, each):
            turn = self.turn[self.at]
            new = self.at == 0 or self.turn[self.at - 1] != turn
            self.at += 1
            if new:
                self.load(turn + 1)
            first = PARTS[parts[-1]][0]
            tokens = sum(PARTS[k][1] for k in parts)

            def body(j, carry):
                if new:
                    fetch(self.runs[turn], turn % 2, j).wait()
                total = jnp.dot(src[first : first + tokens], wbuf[turn % 2, j], preferred_element_type=F32)
                each(total, j, pl.ds(first, tokens), pl.ds(pl.multiple_of(j * COLS, COLS), COLS))
                return carry

            lax.fori_loop(0, steps, body, 0)

    def put(dst, *adds):
        def each(total, j, at, columns):
            for ref in adds:
                total = total + ref[at, columns].astype(F32)
            dst[at, columns] = total.astype(BF16)

        return each

    def resid_in(slot, first, tokens):
        return pltpu.make_async_copy(
            resid.at[:, first : first + tokens], rbuf.at[slot, :, 0:tokens], r_sem.at[0, slot]
        )

    def out_of(slot, first, tokens):
        return pltpu.make_async_copy(
            rbuf.at[slot, :, 0:tokens], out.at[:, first : first + tokens], r_sem.at[1, slot]
        )

    leaving = []

    def final(kind, parts, left, right):
        first = PARTS[parts[-1]][0]
        tokens = sum(PARTS[k][1] for k in parts)
        slot = len(leaving) % 2
        if len(leaving) >= 2:
            out_of(*leaving[-2]).wait()
        resid_in(slot, first, tokens).start()
        leaving.append((slot, first, tokens))
        wait_in(kind, *parts)
        resid_in(slot, first, tokens).wait()
        at = pl.ds(first, tokens)

        def body(j, carry):
            columns = pl.ds(pl.multiple_of(j * COLS, COLS), COLS)
            total = left[at, columns].astype(F32) + right[at, columns].astype(F32) + steer_ref[0:1, columns]
            rbuf[slot, columns, 0:tokens] = (rbuf[slot, columns, 0:tokens].astype(F32) + total.T).astype(BF16)
            return carry

        lax.fori_loop(0, steps, body, 0)
        out_of(slot, first, tokens).start()

    def settle():
        for left in leaving[-2:]:
            out_of(*left).wait()
        leaving.clear()

    blocks_of_channels = channels // LANES

    def load(k, c, slot, act):
        first, tokens = FEATURES[k]
        span = tokens + 256
        lanes = pl.ds(pl.multiple_of(c * LANES, LANES), LANES)
        if first > 0:
            act(pltpu.make_async_copy(
                qkv.at[:, lanes, first - 256 : first + tokens], qbuf.at[slot, :, :, 0:span], q_sem.at[0, slot]
            ))
        else:
            act(pltpu.make_async_copy(
                qkv.at[:, lanes, 0:tokens], qbuf.at[slot, :, :, 256:span], q_sem.at[0, slot]
            ))

            @pl.when(s > 0)
            def _():
                act(pltpu.make_async_copy(rim.at[:, lanes], qbuf.at[slot, :, :, 0:256], q_sem.at[1, slot]))

    def begin(k):
        if FEATURES[k][0] == 0:

            @pl.when(s > 0)
            def _():
                rim_copy.wait_recv()

            @pl.when(s == 0)
            def _():
                qbuf[:, :, :, 0:256] = jnp.zeros((2, 3, LANES, 256), BF16)

        load(k, 0, 0, lambda copy: copy.start())

    def feature(k, start, stop):
        first, tokens = FEATURES[k]
        blocks = (tokens + 256) // LANES
        known, kept = k > 0, k + 1 < len(FEATURES)

        def body(c, carry):
            slot = lax.rem(c, 2)

            @pl.when(c + 1 < blocks_of_channels)
            def _():
                load(k, c + 1, 1 - slot, lambda copy: copy.start())

            load(k, c, slot, lambda copy: copy.wait())
            lanes = pl.ds(pl.multiple_of(c * LANES, LANES), LANES)
            if k == 0:
                split_taps(c, lanes, medium_ref, skip_ref, nine_ref, med)
            for at in range(blocks):
                for i in range(3):
                    if at > 0 if i == 0 else not (known and at == blocks - 1):
                        wide[i, at * LANES : (at + 1) * LANES] = (
                            qbuf[slot, i, :, at * LANES : (at + 1) * LANES].astype(F32).T
                        )
            pieces = filtered(
                blocks, known, kept, short_ref, nine_ref, top, lanes, wide, kv, xs, back, med
            )
            for row, value in pieces:
                y[first + row : first + row + LANES, lanes] = value
            return carry

        lax.fori_loop(start, stop, body, 0)
        if stop == blocks_of_channels and k + 1 < len(FEATURES):
            begin(k + 1)

    def wait_in(kind, *parts):
        for k in parts:
            moving(kind, k).wait_recv()

    def go(kind, *parts):
        for k in parts:
            moving(kind, k).start()

    class Inner:
        def __init__(self, plan):
            self.plan = plan

        def cross(self, *parts):
            wait_in(SUM_IN, *parts)
            self.plan.run(y, parts, put(st1, r1))
            go(ACROSS_OUTER, *parts)

        def far(self, *parts):
            self.plan.run(y, parts, put(st2))

        def far_end(self, *parts):
            wait_in(Y_IN, *parts)
            self.plan.run(yx, parts, put(st2, st2))
            go(ACROSS_INNER, *parts)

        def out(self, *parts):
            wait_in(ACROSS_OUTER, *parts)
            self.plan.run(y, parts, put(st3, rp))
            go(SUM_OUT, *parts)

        def near(self, *parts):
            self.plan.run(y, parts, put(r1))

        def near_end(self, *parts):
            self.plan.run(yx, parts, put(r1, r1))

        def final(self, *parts):
            final(ACROSS_INNER, parts, r1, rq)

    UNIT = {"cross": "fo", "far": "fi", "far_end": 0, "out": "no", "near": "ni", "near_end": 1}
    inner_plan = Plan([UNIT[step[0]] for entry in SCHEDULE for step in entry[3] if step[0] in UNIT])
    inner_work = Inner(inner_plan)

    class Outer:
        def __init__(self, plan):
            self.plan = plan

        def sum(self, *parts):
            self.plan.run(y, parts, put(st1))

        def go_sum(self, *parts):
            go(SUM_IN, *parts)

        def go_y(self, *parts):
            go(Y_IN, *parts)

        def go_w(self, g):
            for h in range(2):
                w_inward(g, h).start()

        def out(self, *parts):
            self.plan.run(y, parts, put(rp))

        def final(self, *parts):
            final(SUM_OUT, parts, rp, r1)

    OUTER_UNIT = {"sum": "fo", "out": "no"}
    outer_plan = Plan([OUTER_UNIT[step[0]] for entry in SCHEDULE for step in entry[4] if step[0] in OUTER_UNIT])
    outer_work = Outer(outer_plan)

    begin(0)

    @pl.when(outer)
    def _():
        for h in range(2):
            w_inward(0, h).start()
        outer_plan.load(0)

    @pl.when(inner)
    def _():
        inner_plan.load(0)

    short_ref[...] = short_taps[...].astype(F32)
    for number, (k, start, stop, inner_steps, outer_steps) in enumerate(SCHEDULE):
        feature(k, start, stop)
        ending = number == len(SCHEDULE) - 1

        @pl.when(inner)
        def _():
            for step in inner_steps:
                if step[0] == "plane":
                    relay_plane(*step[1:])
                elif step[0] == "core":
                    relay_core(*step[1:])
                else:
                    getattr(inner_work, step[0])(*step[1:])
            if ending:
                settle()
                for part in range(len(PARTS)):
                    moving(ACROSS_OUTER, part).wait_send()
                    moving(ACROSS_INNER, part).wait_send()
                    moving(SUM_OUT, part).wait_send()
                for g in range(2):
                    for h in range(2):
                        for i in range(3):
                            w_plane(g, h, i).wait_send()
                        for i in range(4):
                            w_core(g, h, i).wait_send()

        @pl.when(outer)
        def _():
            for step in outer_steps:
                getattr(outer_work, step[0])(*step[1:])
            if ending:
                settle()
                for part in range(len(PARTS)):
                    moving(SUM_IN, part).wait_send()
                    moving(Y_IN, part).wait_send()
                for g in range(2):
                    for h in range(2):
                        w_inward(g, h).wait_send()

    pl.when(s < 7)(rim_copy.wait_send)


SCHEDULE = (
    (0, 0, 11, (("plane", 0, 0),), ()),
    (0, 11, 16, (), (("sum", 0, 1), ("go_sum", 0, 1))),
    (1, 0, 8, (("plane", 0, 1),), ()),
    (1, 8, 15, (("cross", 0),), ()),
    (1, 15, 16, (), (("sum", 2), ("go_sum", 2), ("go_y", 0, 1, 2))),
    (2, 0, 2, (("cross", 1),), ()),
    (2, 2, 11, (("core", 0, 0), ("cross", 2)), ()),
    (2, 11, 16, (("core", 0, 1), ("far", 0, 1, 2), ("far_end", 0, 1)), (("sum", 3, 4), ("go_sum", 3, 4))),
    (3, 0, 6, (("far_end", 2), ("cross", 3)), ()),
    (3, 6, 11, (("cross", 4), ("out", 0, 1, 2)), ()),
    (3, 11, 16, (), (("sum", 5, 6), ("go_sum", 5, 6))),
    (4, 0, 4, (("cross", 5),), ()),
    (4, 4, 12, (("cross", 6),), ()),
    (4, 12, 16, (
        ("far", 3, 4), ("near", 0, 1, 2), ("far_end", 3), ("out", 3, 4), ("near", 3, 4), ("far_end", 4), ("plane", 1, 0), ("far", 5, 6), ("near", 5, 6),
        ("plane", 1, 1), ("out", 5, 6), ("cross", 7), ("core", 1, 0), ("cross", 8), ("cross", 9), ("near", 7, 8, 9), ("far_end", 5), ("out", 7, 8, 9),
        ("far", 7, 8, 9), ("core", 1, 1), ("far_end", 6), ("near_end", 0, 1, 2), ("near_end", 3, 4), ("final", 0, 1, 2), ("far_end", 7), ("near_end", 5, 6), ("far_end", 8), ("final", 3, 4),
        ("far_end", 9), ("near_end", 7, 8, 9), ("final", 5, 6), ("final", 7), ("final", 8, 9),
    ), (
        ("sum", 7, 8, 9), ("go_y", 3, 4), ("go_w", 1), ("go_sum", 7, 8, 9), ("go_y", 5, 6, 7, 8, 9),
        ("out", 0, 1, 2), ("out", 3, 4), ("out", 5, 6), ("out", 7, 8, 9),
        ("final", 0, 1, 2), ("final", 3, 4), ("final", 5, 6), ("final", 7, 8, 9),
    )),
)


def lined(qkv, short_taps, medium_taps, skip_gain, w_out, resid, steer):
    channels, slab = qkv.shape[1:]
    width = resid.shape[0]
    whole = pl.BlockSpec(memory_space=pltpu.VMEM)
    anywhere = pl.BlockSpec(memory_space=pl.ANY)
    token = lambda: pltpu.VMEM((slab, channels), BF16)
    dma = pltpu.SemaphoreType.DMA
    span = 512
    return pl.pallas_call(
        line_kernel,
        in_specs=[anywhere] * 3 + [whole] * 4,
        out_specs=[anywhere] * 4,
        out_shape=[
            jax.ShapeDtypeStruct(resid.shape, BF16),
            jax.ShapeDtypeStruct((channels, width), BF16),
            jax.ShapeDtypeStruct((channels, width), BF16),
            jax.ShapeDtypeStruct((3, channels, 256), BF16),
        ],
        scratch_shapes=[token() for _ in range(8)]
        + [
            pltpu.VMEM((2, width // COLS, channels, COLS), BF16),
            pltpu.VMEM((2, 3, LANES, span), BF16),
            pltpu.VMEM((2, width, 256), BF16),
            pltpu.VMEM((3, STAPS, channels), F32),
            pltpu.VMEM((9 * PHASE, channels), F32),
            pltpu.VMEM((LANES, channels), F32),
            pltpu.VMEM((3, span, LANES), F32),
            pltpu.VMEM((span - LANES, LANES), F32),
            pltpu.VMEM((9, EDGE + (span - LANES) // 4, LANES), F32),
            pltpu.VMEM((EDGE + 64, LANES), F32),
            pltpu.VMEM((256, LANES), F32),
            dma((5, len(PARTS))),
            dma((5, len(PARTS))),
            dma((2, 2, 8)),
            dma((2, 2, 8)),
            dma,
            dma,
            dma((2, width // COLS)),
            dma((2, 2)),
            dma((2, 2)),
        ],
        compiler_params=pltpu.CompilerParams(
            collective_id=0, has_side_effects=True, vmem_limit_bytes=VMEM_LIMIT
        ),
        cost_estimate=pl.CostEstimate(
            flops=12 * channels * slab * width, bytes_accessed=20 * channels * width, transcendentals=0
        ),
    )(qkv, w_out, resid, jnp.swapaxes(short_taps, 1, 2), medium_taps, skip_gain[None], steer[None])[0]


def solution(mesh):
    line = mesh.shape["mp"] == 4 and mesh.shape["seq"] == 8
    return jax.shard_map(
        lined if line else shards,
        mesh=mesh,
        in_specs=(
            P(None, "mp", "seq"),
            P(None, "mp", None),
            P("mp", None),
            P("mp"),
            P("mp", None),
            P("mp", "seq"),
            P("mp"),
        ),
        out_specs=P("mp", "seq"),
        check_vma=False,
    )
```
